256 devices in a mesh: ens: 4 (over x_lo, core), grid: 64 (over z, y, x_hi).
Axes of the slice: x: 4 (x_hi: 2, x_lo: 2; x = x_hi * 2 + x_lo), y: 4, z: 8, core: 2. Of those that a mesh axis runs over, the one named last changes fastest.
Arguments:
- latent: bfloat16 [8, 16384, 1024], P('ens', 'grid'), may hold values from -6 to 6
- edge_src: int32 [16384, 3], P('grid'), may hold values from 0 to 16383, as said below
- counts: int32 [64], replicated, may hold values from 128 to 256, as said below
- targets: float32 [100, 16384], P(None, 'grid'), may hold values from -4 to 4
- area: float32 [16384], P('grid'), may hold values from 0.3 to 3
- var_weight: float32 [100], replicated, may hold values from 0.1 to 1
- w_in: bfloat16 [1024, 1024], replicated, may hold values from -0.1875 to 0.1875
- b_in: float32 [1024], replicated, may hold values from -3 to 3
- w_out: bfloat16 [1024, 100], replicated, may hold values from -0.1875 to 0.1875
- b_out: float32 [100], replicated, may hold values from -3 to 3
Outputs:
- grad_latent: bfloat16 [8, 16384, 1024], P('ens', 'grid')
- grad_w_in: float32 [1024, 1024], replicated
- grad_b_in: float32 [1024], replicated
- grad_w_out: float32 [1024, 100], replicated
- grad_b_out: float32 [100], replicated
- loss: float32 [], replicated
The draws below stay inside these ranges and needn't reach their ends.
Inputs may be any that keep to these rules, and one draw needn't show every extreme that they name: `edge_src`: every edge of a grid point in tile s (rows s * 256 to (s + 1) * 256 - 1) names a latent node of tile s - 1, s or s + 1 taken cyclically over 64 tiles, latent tile t holding nodes t * 256 to (t + 1) * 256 - 1. The valid points of tile s are its first counts[s].
All inputs are finite; a program needn't handle non-finite values.
Results may differ from the reference program's by a relative error of at most 0.0079.
Values may be sent and summed in bfloat16 or wider, within the bound.
No kernel may reach another device: no remote copies, remote signals or barrier semaphores. Data moves between devices by JAX's collectives and lax.ppermute only.
A program may use at most 128 MiB of HBM per device.

```python
import math
import jax
import jax.numpy as jnp
from jax import lax

H = 1024
V = 100
K_EDGES = 3
G_DEV = 256
L_DEV = 256
MEMBERS = 8
SHARDS = 64
GRID = 16384
LATENT = 16384


def draw_edge_src(key, part):
    key = jax.random.fold_in(key, 11)
    tiles = jnp.arange(GRID, dtype=jnp.int32) // G_DEV
    offsets = jax.random.randint(key, (GRID, K_EDGES), -L_DEV, 2 * L_DEV, dtype=jnp.int32)
    source = jnp.mod(tiles[:, None] * L_DEV + offsets, LATENT).astype(jnp.int32)
    source = source.at[0, 0].set(LATENT - 1)
    source = source.at[0, 1].set(0)
    return source


def draw_counts(key, part):
    key = jax.random.fold_in(key, 23)
    values = jax.random.randint(key, (SHARDS,), G_DEV // 2, G_DEV + 1, dtype=jnp.int32)
    values = values.at[0].set(G_DEV)
    values = values.at[SHARDS - 1].set(G_DEV // 2)
    return values


def level_of(key, dims, split, smallest, largest):
    loudness, own = 1.0, jax.random.fold_in(key, 6)
    for dim, blocks in split:
        steps = jnp.exp(jax.random.uniform(jax.random.fold_in(own, dim), (blocks,), jnp.float32, smallest / len(split), largest / len(split)))
        loudness = loudness * jnp.repeat(steps, dims[dim] // blocks).reshape([-1 if axis == dim else 1 for axis in range(len(dims))])
    return loudness


def centred(rng, extent, scale, limit, shards=(), kind=jnp.bfloat16):
    entries = jax.random.normal(rng, extent, jnp.float32) * scale
    if len(shards) > 0:
        entries = level_of(rng, extent, shards, -0.22, 0.18) * entries
    return jnp.clip(entries, min=-limit, max=limit).astype(kind)


def setup_inputs(seed: int = 0) -> dict:
    arg_keys = jax.random.split(jax.random.key(seed), 11)
    return {
        "latent": centred(arg_keys[0], (MEMBERS, LATENT, H), 1.0, 6.0, ((0, 4), (1, 64))),
        "edge_src": draw_edge_src(jax.random.fold_in(arg_keys[10], 71), 0),
        "counts": draw_counts(jax.random.fold_in(arg_keys[10], 71), 0),
        "targets": centred(arg_keys[3], (V, GRID), 0.5, 4.0, ((1, 64),), jnp.float32),
        "area": jnp.clip(jnp.exp(math.log(3.0) - 2.3025851 * jax.random.uniform(arg_keys[4], (GRID,), jnp.float32) ** level_of(arg_keys[4], (GRID,), ((0, 64),), -0.2, 0.2)), 0.3, 3.0),
        "var_weight": jnp.clip(jnp.exp(jax.random.uniform(arg_keys[5], (V,), jnp.float32, math.log(0.1), math.log(1.0))), 0.1, 1.0),
        "w_in": centred(arg_keys[6], (H, H), H ** -0.5, 0.1875),
        "b_in": centred(arg_keys[7], (H,), 0.5, 3.0, (), jnp.float32),
        "w_out": centred(arg_keys[8], (H, V), H ** -0.5, 0.1875),
        "b_out": centred(arg_keys[9], (V,), 0.5, 3.0, (), jnp.float32),
    }


smooth_sq = 0.0025
smooth_width = 0.05

def smooth(d):
    return jnp.sqrt(d * d + smooth_sq) - smooth_width

def smooth_slope(d):
    return d / jnp.sqrt(d * d + smooth_sq)

def gelu_value(v):
    return 0.5 * v * (1.0 + lax.erf(v * 0.7071067811865476))

def gelu_slope(v):
    return 0.5 * (1.0 + lax.erf(v * 0.7071067811865476)) + v * jnp.exp(-0.5 * v * v) * 0.3989422804014327

def reference(latent, edge_src, counts, targets, area, var_weight, w_in, b_in, w_out, b_out):
    members = latent.shape[0]
    w_in32 = w_in.astype(jnp.float32)
    w_out32 = w_out.astype(jnp.float32)

    def one_tile(carry, tile):
        gw_in, gb_in, gw_out, gb_out, total, grad_lat = carry
        start = (tile * G_DEV).astype(jnp.int32)
        src = lax.dynamic_slice_in_dim(edge_src, start, G_DEV, 0)
        tgt = lax.dynamic_slice_in_dim(targets, start, G_DEV, 1)
        area_t = lax.dynamic_slice_in_dim(area, start, G_DEV, 0)
        valid = (jnp.arange(G_DEV, dtype=jnp.int32) < counts[tile]).astype(jnp.float32)
        wgt = var_weight[:, None] * (area_t * valid)[None, :]
        acc = jnp.zeros((members, G_DEV, H), jnp.float32)
        for k in range(K_EDGES):
            acc = acc + latent[:, src[:, k]].astype(jnp.float32)
        features = (acc / K_EDGES).astype(jnp.bfloat16)
        pre = jnp.einsum('mgh,hk->mgk', features.astype(jnp.float32), w_in32) + b_in
        hidden = gelu_value(pre).astype(jnp.bfloat16)
        pred = jnp.einsum('mgh,hv->mvg', hidden.astype(jnp.float32), w_out32) + b_out[None, :, None]
        dsum = jnp.zeros_like(pred)
        ssum = jnp.zeros_like(pred)
        for j in range(members):
            diff = pred - pred[j][None]
            dsum = dsum + smooth_slope(diff)
            ssum = ssum + smooth(diff)
        err = pred - tgt[None]
        mm = float(members)
        total = total + jnp.sum(wgt[None] * (smooth(err) / mm - ssum / (2.0 * mm * (mm - 1.0))))
        grad_pred = wgt[None] * (smooth_slope(err) / mm - dsum / (mm * (mm - 1.0)))
        gb_out = gb_out + lax.optimization_barrier(jnp.sum(grad_pred, axis=(0, 2)))
        dpred = grad_pred.astype(jnp.bfloat16).astype(jnp.float32)
        gw_out = gw_out + jnp.einsum('mgh,mvg->hv', hidden.astype(jnp.float32), dpred)
        dhid = jnp.einsum('mvg,hv->mgh', dpred, w_out32)
        dpre = (dhid * gelu_slope(pre)).astype(jnp.bfloat16).astype(jnp.float32)
        gb_in = gb_in + lax.optimization_barrier(jnp.sum(dpre, axis=(0, 1)))
        gw_in = gw_in + jnp.einsum('mgh,mgk->hk', features.astype(jnp.float32), dpre)
        dfeat = jnp.einsum('mgk,hk->mgh', dpre, w_in32) / K_EDGES
        for k in range(K_EDGES):
            grad_lat = grad_lat.at[:, src[:, k]].add(dfeat)
        return ((gw_in, gb_in, gw_out, gb_out, total, grad_lat), None)
    init = (jnp.zeros((H, H), jnp.float32), jnp.zeros((H,), jnp.float32), jnp.zeros((H, V), jnp.float32), jnp.zeros((V,), jnp.float32), jnp.zeros((), jnp.float32), jnp.zeros((members, LATENT, H), jnp.float32))
    result, _ = lax.scan(one_tile, init, jnp.arange(SHARDS, dtype=jnp.int32))
    gw_in, gb_in, gw_out, gb_out, total, grad_lat = result
    return (grad_lat.astype(jnp.bfloat16), gw_in, gb_in, gw_out, gb_out, total)
```

```python
import jax
import jax.numpy as jnp
from jax import lax
from jax.sharding import Mesh, PartitionSpec as P

smooth_sq = 0.0025
smooth_width = 0.05
bf16 = jnp.bfloat16
f32 = jnp.float32

ENS = ("xl", "c")
GRID = ("z", "y", "xh")
GROUP = ("xh", "xl", "c")
PLANE = ("y", "xh", "xl")
WIDE = 1152


def gelu_parts(v):
    cdf = 0.5 * (1.0 + lax.erf(v * 0.7071067811865476))
    slope = cdf + v * jnp.exp(-0.5 * v * v) * 0.3989422804014327
    return v * cdf, slope


def ring(shift_odd, shift_even):
    n = 64
    return [(i, (i + (shift_odd if i % 2 else shift_even)) % n) for i in range(n)]


SWAP = ring(-1, 1)
SAME = ring(2, -2)
DIAG = ring(1, -1)


def back(perm):
    return [(b, a) for a, b in perm]


def spread(block, axes):
    n = lax.axis_size(axes)
    many = jnp.broadcast_to(block[None], (n,) + block.shape)
    return lax.all_to_all(many, axes, split_axis=0, concat_axis=0, tiled=True)


def resplit(total):
    col = lax.broadcasted_iota(jnp.int32, total.shape, total.ndim - 1)
    both = total[..., WIDE - 2 : WIDE - 1] + total[..., WIDE - 1 : WIDE]
    high = lax.reduce_precision(both, 8, 7)
    low = both - high
    return jnp.where(
        col == WIDE - 2, high, jnp.where(col == WIDE - 1, low, total)
    ).astype(bf16)


def reduced(grads):
    half = grads.shape[0] // 2
    core = lax.axis_index("c")
    mine = lax.dynamic_slice_in_dim(grads, core * half, half, 0)
    other = lax.dynamic_slice_in_dim(grads, (1 - core) * half, half, 0)
    got = lax.ppermute(resplit(other), "c", [(0, 1), (1, 0)])
    part = resplit(mine + got.astype(f32))
    n = lax.axis_size(PLANE)
    part = lax.all_to_all(
        part.reshape(n, half // n, WIDE), PLANE, split_axis=0, concat_axis=0, tiled=True
    )
    part = resplit(jnp.sum(part.astype(f32), axis=0))
    part = spread(part, "z")
    part = resplit(jnp.sum(part.astype(f32), axis=0))
    part = spread(part, PLANE).reshape(half, WIDE)
    got = lax.ppermute(part, "c", [(0, 1), (1, 0)])
    low = jnp.where(core == 0, part, got)
    high = jnp.where(core == 0, got, part)
    return jnp.concatenate([low, high], axis=0)


def body(latent, edge_src, counts, targets, area, var_weight, w_in, b_in, w_out, b_out):
    l_tile, width = latent.shape[1:]
    g_tile, k_edges = edge_src.shape
    n_vars = w_out.shape[1]
    h = lax.axis_index("xh")
    pair = lax.axis_index(("z", "y"))
    tile = 2 * pair + h
    quarter = lax.axis_index(ENS)
    members = 8
    pts = g_tile // 4

    own = lax.dynamic_index_in_dim(latent, h, 0, keepdims=False)
    oth = lax.dynamic_index_in_dim(latent, 1 - h, 0, keepdims=False)
    edges_there = lax.ppermute(edge_src, GRID, SWAP)
    swapped = lax.ppermute(oth, GRID, SWAP)
    diag = lax.ppermute(oth, GRID, DIAG)
    same = lax.ppermute(own, GRID, SAME)

    edges = jnp.where(
        h == 0,
        jnp.concatenate([edge_src, edges_there], axis=0),
        jnp.concatenate([edges_there, edge_src], axis=0),
    )
    step = edges // l_tile - 2 * pair
    block = jnp.mod(jnp.where(h == 0, step, 1 - step), 4)
    local = block * l_tile + jnp.mod(edges, l_tile)
    nodes = lax.broadcasted_iota(jnp.int32, (2 * g_tile, 4 * l_tile), 1)
    pick = jnp.zeros((2 * g_tile, 4 * l_tile), f32)
    for k in range(k_edges):
        pick = pick + (local[:, k : k + 1] == nodes).astype(f32)
    pick = pick.astype(bf16)

    window = jnp.concatenate([own, swapped, same, diag], axis=0)
    features = (jnp.dot(pick, window, preferred_element_type=f32) / k_edges).astype(bf16)
    pre = jnp.dot(features, w_in, preferred_element_type=f32) + b_in
    hidden, slope = gelu_parts(pre)
    hidden = hidden.astype(bf16)
    pred = jnp.dot(hidden, w_out, preferred_element_type=f32) + b_out

    pred = lax.all_to_all(
        pred.reshape(members, pts, n_vars), GROUP, split_axis=0, concat_axis=0, tiled=True
    )
    start = quarter * pts
    point = start + jnp.arange(pts, dtype=jnp.int32)
    valid = (point < counts[tile]).astype(f32)
    wgt = (lax.dynamic_slice_in_dim(area, start, pts, 0) * valid)[:, None] * var_weight[None, :]
    aim = lax.dynamic_slice_in_dim(targets, start, pts, 1).T
    slopes = [None] * members
    gaps = jnp.zeros((pts, n_vars), f32)
    hits = jnp.zeros((pts, n_vars), f32)
    grads = []
    pair_sum = [jnp.zeros((pts, n_vars), f32) for _ in range(members)]
    for i in range(members):
        for j in range(i + 1, members):
            d = pred[i] - pred[j]
            sq = d * d + smooth_sq
            r = lax.rsqrt(sq)
            gaps = gaps + (sq * r - smooth_width)
            pair_sum[i] = pair_sum[i] + d * r
            pair_sum[j] = pair_sum[j] - d * r
    mm = float(members)
    for i in range(members):
        d = pred[i] - aim
        sq = d * d + smooth_sq
        r = lax.rsqrt(sq)
        hits = hits + (sq * r - smooth_width)
        grads.append(wgt * (d * r / mm - pair_sum[i] / (mm * (mm - 1.0))))
    total = jnp.sum(wgt * (hits / mm - gaps / (mm * (mm - 1.0))))
    grad_pred = jnp.stack(grads)
    gb_out = jnp.sum(grad_pred, axis=(0, 1))
    dpred = lax.all_to_all(
        grad_pred.astype(bf16), GROUP, split_axis=0, concat_axis=0, tiled=True
    ).reshape(members * pts, n_vars)

    dhid = lax.dot_general(dpred, w_out, (((1,), (1,)), ((), ())), preferred_element_type=f32)
    dpre = (dhid * slope).astype(bf16)
    gb_in = jnp.sum(dpre.astype(f32), axis=0)
    gw_out = lax.dot_general(hidden, dpred, (((0,), (0,)), ((), ())), preferred_element_type=f32)
    gw_in = lax.dot_general(features, dpre, (((0,), (0,)), ((), ())), preferred_element_type=f32)
    small = jnp.concatenate([gb_out, total[None], jnp.zeros((width - n_vars - 1,), f32)])
    gap = jnp.zeros((width, WIDE - width - n_vars - 3), f32)
    zero = jnp.zeros((width, 1), f32)
    grads = jnp.concatenate([gw_in, gw_out, gap, gb_in[:, None], small[:, None], zero], axis=1)

    dfeat = lax.dot_general(dpre, w_in, (((1,), (1,)), ((), ())), preferred_element_type=f32)
    dfeat = (dfeat / k_edges).astype(bf16)
    dwin = lax.dot_general(pick, dfeat, (((0,), (0,)), ((), ())), preferred_element_type=f32)
    d_own = dwin[:l_tile]
    sent = dwin[l_tile:].astype(bf16)
    to_swap = lax.ppermute(sent[:l_tile], GRID, back(SWAP))
    to_same = lax.ppermute(sent[l_tile : 2 * l_tile], GRID, back(SAME))
    to_diag = lax.ppermute(sent[2 * l_tile :], GRID, back(DIAG))
    d_own = (d_own + to_same.astype(f32)).astype(bf16)
    d_oth = (to_swap.astype(f32) + to_diag.astype(f32)).astype(bf16)
    grad_latent = jnp.stack([jnp.where(h == 0, d_own, d_oth), jnp.where(h == 0, d_oth, d_own)])

    full = reduced(grads).astype(f32)
    small = full[:, WIDE - 2] + full[:, WIDE - 1]
    return (
        grad_latent,
        full[:, :width],
        full[:, WIDE - 3],
        full[:, width : width + n_vars],
        small[:n_vars],
        small[n_vars],
    )


def solution(mesh):
    fine = Mesh(mesh.devices.reshape(2, 2, 8, 4, 2), ENS + GRID)
    in_specs = (
        P(ENS, GRID, None),
        P(GRID, None),
        P(),
        P(None, GRID),
        P(GRID),
        P(),
        P(),
        P(),
        P(),
        P(),
    )
    out_specs = (P(ENS, GRID, None), P(), P(), P(), P(), P())
    return jax.shard_map(body, mesh=fine, in_specs=in_specs, out_specs=out_specs, check_vma=False)
```

```python
import jax
import jax.numpy as jnp
from jax import lax
from jax.experimental import pallas as pl
from jax.experimental.pallas import tpu as pltpu
from jax.sharding import Mesh, PartitionSpec as P

smooth_sq = 0.0025
smooth_width = 0.05
bf16 = jnp.bfloat16
f32 = jnp.float32

ENS = ("xl", "c")
GRID = ("z", "y", "xh")
GROUP = ("xh", "xl", "c")
PLANE = ("y", "xh", "xl")
MEMBERS = 8
H = 1024
LANES = 128
CHUNK = 256
STEPS = H // CHUNK
ROWS = H + LANES
ROW_GROUPS = 4
PART = ROWS // ROW_GROUPS
PARTS = 16
GB_IN, HIGH, LOW = 100, 101, 102
HIGH_IN_PART = H + HIGH - 3 * PART


def dot(a, b, dims=((1,), (0,))):
    return lax.dot_general(a, b, (dims, ((), ())), preferred_element_type=f32)


def call(kernel, name, flops=0, nbytes=0, trans=0, **kw):
    return pl.pallas_call(
        kernel,
        name=name,
        cost_estimate=pl.CostEstimate(flops=flops, bytes_accessed=nbytes, transcendentals=trans),
        compiler_params=pltpu.CompilerParams(vmem_limit_bytes=24 * 1024 * 1024),
        **kw,
    )


def near(*xs):
    return [pltpu.with_memory_space_constraint(x, pltpu.VMEM) for x in xs]


def far(x):
    return pltpu.with_memory_space_constraint(x, pltpu.HBM)


def out(shape, dtype):
    return pltpu.VMEM(shape, dtype)


def ring(shift_odd, shift_even):
    n = 64
    return [(i, (i + (shift_odd if i % 2 else shift_even)) % n) for i in range(n)]


SWAP = ring(-1, 1)
SAME = ring(2, -2)
DIAG = ring(1, -1)


def back(perm):
    return [(b, a) for a, b in perm]


def a2a(x, axes):
    return lax.all_to_all(x, axes, split_axis=0, concat_axis=0, tiled=True)


def forward_kernel(pick, own, swp, same, diag, w_in, b_in, w_out, b_out, feats_t, hid, slope, pred, w_here, sem):
    n = own.shape[0]
    copy = pltpu.make_async_copy(w_in, w_here, sem)
    copy.start()
    total = dot(pick[:, :n], own[...])
    for k, ref in enumerate((swp, same, diag)):
        total = total + dot(pick[:, (k + 1) * n : (k + 2) * n], ref[...])
    feats = (total / 3.0).astype(bf16)
    feats_t[...] = feats.T
    copy.wait()
    v = dot(feats, w_here[...]) + b_in[...]
    cdf = 0.5 * (1.0 + lax.erf(v * 0.7071067811865476))
    slope[...] = (cdf + v * jnp.exp(-0.5 * v * v) * 0.3989422804014327).astype(bf16)
    h = (v * cdf).astype(bf16)
    hid[...] = h
    p = dot(h, w_out[...]) + b_out[...]
    pts = pred.shape[1]
    for i in range(MEMBERS):
        pred[i] = p[i * pts : (i + 1) * pts]


def forward(pick, own, swp, same, diag, w_in, b_in, w_out, b_out):
    m = pick.shape[0]
    return call(
        forward_kernel,
        "forward",
        flops=2 * m * H * (2 * H + LANES),
        nbytes=12 * 2**20,
        trans=2 * m * H,
        in_specs=[pl.BlockSpec(memory_space=pltpu.VMEM)] * 5
        + [pl.BlockSpec(memory_space=pl.ANY)]
        + [pl.BlockSpec(memory_space=pltpu.VMEM)] * 3,
        scratch_shapes=[pltpu.VMEM((H, H), bf16), pltpu.SemaphoreType.DMA],
        out_shape=[
            out((H, m), bf16),
            out((m, H), bf16),
            out((m, H), bf16),
            jax.ShapeDtypeStruct((MEMBERS, m // MEMBERS, LANES), f32),
        ],
    )(*near(pick, own, swp, same, diag), far(w_in), *near(b_in, w_out, b_out))


def crps_kernel(pred, aim, wgt, dpred, small):
    mm = float(MEMBERS)
    pts = pred.shape[1]
    gb = jnp.zeros((1, LANES), f32)
    loss = jnp.zeros((1, LANES), f32)
    for r in range(0, pts, 16):
        p = [pred[i, r : r + 16, :] for i in range(MEMBERS)]
        pair = [jnp.zeros((16, LANES), f32) for _ in range(MEMBERS)]
        gaps = jnp.zeros((16, LANES), f32)
        hits = jnp.zeros((16, LANES), f32)
        for i in range(MEMBERS):
            for j in range(i + 1, MEMBERS):
                d = p[i] - p[j]
                sq = d * d + smooth_sq
                inv = lax.rsqrt(sq)
                gaps = gaps + (sq * inv - smooth_width)
                pair[i] = pair[i] + d * inv
                pair[j] = pair[j] - d * inv
        w = wgt[r : r + 16, :]
        t = aim[r : r + 16, :]
        g_sum = jnp.zeros((16, LANES), f32)
        for i in range(MEMBERS):
            d = p[i] - t
            sq = d * d + smooth_sq
            inv = lax.rsqrt(sq)
            hits = hits + (sq * inv - smooth_width)
            g = w * (d * inv / mm - pair[i] / (mm * (mm - 1.0)))
            g_sum = g_sum + g
            dpred[i, r : r + 16, :] = g.astype(bf16)
        gb = gb + jnp.sum(g_sum, axis=0, keepdims=True)
        loss = loss + jnp.sum(w * (hits / mm - gaps / (mm * (mm - 1.0))), axis=0, keepdims=True)
    small[:, :LANES] = gb
    small[:, LANES:] = loss


def crps(pred, aim, wgt):
    pts = aim.shape[0]
    return call(
        crps_kernel,
        "crps",
        flops=40 * 36 * pts * LANES,
        nbytes=2**19,
        trans=36 * pts * LANES,
        out_shape=[
            jax.ShapeDtypeStruct((MEMBERS, pts, LANES), bf16),
            out((1, 2 * LANES), f32),
        ],
    )(*near(pred, aim, wgt))


def packed(half, feats_t, dpre, dpred, hid, small):
    cols = pl.ds(pl.multiple_of(half * (H // 2), H // 2), H // 2)
    d = dpre[:, cols]
    gb_in = jnp.sum(d.astype(f32), axis=0, keepdims=True)
    foot = dot(dpred[...], hid[:, cols], ((0,), (0,)))
    row = lax.broadcasted_iota(jnp.int32, foot.shape, 0)
    s = jnp.concatenate([small[...], jnp.zeros_like(small[...])], axis=1)
    s = jnp.where(half == 0, s, 0.0)
    high = s.astype(bf16).astype(f32)
    foot = jnp.where(row == GB_IN, gb_in, foot)
    foot = jnp.where(row == HIGH, high, foot)
    foot = jnp.where(row == LOW, s - high, foot)
    main = dot(feats_t[...], d)
    for g in range(ROW_GROUPS):
        lanes = slice(g * LANES, (g + 1) * LANES)
        for r in range(ROW_GROUPS):
            block = main[r * PART : (r + 1) * PART, lanes]
            if r == ROW_GROUPS - 1:
                block = jnp.concatenate([block, foot[:, lanes]], axis=0)
            yield g * ROW_GROUPS + r, block


def backward_kernel(core, dpred, w_out, slope, hid, feats_t, small, dpre, send):
    d = dot(dpred[...], w_out[...], ((1,), (1,))) * slope[...].astype(f32)
    dpre[...] = d.astype(bf16)
    for i, block in packed(1 - core[0], feats_t, dpre, dpred, hid, small):
        send[i] = block.astype(bf16)


def backward(core, dpred, w_out, slope, hid, feats_t, small):
    m = dpred.shape[0]
    return call(
        backward_kernel,
        "backward",
        flops=m * H * (H + 4 * LANES),
        nbytes=6 * 2**20,
        in_specs=[pl.BlockSpec(memory_space=pltpu.SMEM)]
        + [pl.BlockSpec(memory_space=pltpu.VMEM)] * 6,
        out_shape=[out((m, H), bf16), out((PARTS, PART, LANES), bf16)],
    )(core, *near(dpred, w_out, slope, hid, feats_t, small))


def latent_kernel(dpre, w_in, pick_t, own, swp, same, diag):
    d = (dot(dpre[...], w_in[...], ((1,), (1,))) / 3.0).astype(bf16)
    n = own.shape[0]
    for k, ref in enumerate((own, swp, same, diag)):
        ref[...] = dot(pick_t[k * n : (k + 1) * n, :], d).astype(ref.dtype)


def latent_grads(dpre, w_in, pick_t):
    m = dpre.shape[0]
    n = pick_t.shape[0] // 4
    return call(
        latent_kernel,
        "latent_grads",
        flops=4 * m * H * H,
        nbytes=8 * 2**20,
        out_shape=[out((n, H), f32)] + [jax.ShapeDtypeStruct((n, H), bf16)] * 3,
    )(*near(dpre, w_in, pick_t))


def resplit(total):
    row = lax.broadcasted_iota(jnp.int32, total.shape, 0)
    both = total[HIGH_IN_PART : HIGH_IN_PART + 1] + total[HIGH_IN_PART + 1 : HIGH_IN_PART + 2]
    high = both.astype(bf16).astype(f32)
    total_high = jnp.where(row == HIGH_IN_PART, high, total)
    return jnp.where(row == HIGH_IN_PART + 1, both - high, total_high).astype(bf16)


def pair_kernel(core, dpred, dpre, hid, feats_t, small, got, part):
    for i, block in packed(core[0], feats_t, dpre, dpred, hid, small):
        total = block + got[i].astype(f32)
        if i % ROW_GROUPS == ROW_GROUPS - 1:
            total = resplit(total)
        part[i] = total.astype(bf16)


def pair_sum(core, dpred, dpre, hid, feats_t, small, got):
    m = dpred.shape[0]
    return call(
        pair_kernel,
        "pair_sum",
        flops=m * H * (H + 2 * LANES),
        nbytes=6 * 2**20,
        in_specs=[pl.BlockSpec(memory_space=pltpu.SMEM)]
        + [pl.BlockSpec(memory_space=pltpu.VMEM)] * 6,
        out_shape=jax.ShapeDtypeStruct(got.shape, bf16),
    )(core, *near(dpred, dpre, hid, feats_t, small, got))


def total_kernel(group, parts, copies):
    total = parts[0].astype(f32)
    for i in range(1, parts.shape[0]):
        total = total + parts[i].astype(f32)
    last = group[0] == ROW_GROUPS - 1
    done = jnp.where(last, resplit(total).astype(f32), total).astype(bf16)
    for i in range(copies.shape[0]):
        copies[i] = done


def total_and_spread(group, parts, copies):
    n = parts.shape[0]
    return call(
        total_kernel,
        "total",
        flops=n * PART * LANES,
        nbytes=2 * (n + copies) * PART * LANES,
        in_specs=[
            pl.BlockSpec(memory_space=pltpu.SMEM),
            pl.BlockSpec(memory_space=pltpu.VMEM),
        ],
        out_shape=jax.ShapeDtypeStruct((copies, PART, LANES), bf16),
    )(group, *near(parts))


def unpack_kernel(core, mine, got, gw_in, gw_out_t, gb_in, gb_out, loss):
    j = pl.program_id(0)

    def put(ref):
        for g in range(2):
            lanes = slice(g * LANES, (g + 1) * LANES)
            base = g * ROW_GROUPS
            for r in range(ROW_GROUPS - 1):
                gw_in[r * PART : (r + 1) * PART, lanes] = ref[base + r].astype(f32)
            r = ROW_GROUPS - 1
            gw_in[r * PART :, lanes] = ref[base + r, : H - r * PART, :].astype(f32)
            foot = ref[base + r, H - r * PART :, :].astype(f32)
            gw_out_t[:, lanes] = foot[:GB_IN]
            gb_in[:, lanes] = foot[GB_IN : GB_IN + 1]
            small = foot[HIGH : HIGH + 1] + foot[LOW : LOW + 1]

            @pl.when(j == 0)
            def _():
                if g == 0:
                    gb_out[...] = small[:, :GB_IN]
                else:
                    loss[...] = jnp.sum(small, axis=1, keepdims=True)

    here = j // 2 == core[0]

    @pl.when(here)
    def _():
        put(mine)

    @pl.when(jnp.logical_not(here))
    def _():
        put(got)


def unpack(core, mine, got):
    block = (2 * ROW_GROUPS, PART, LANES)
    cols = lambda j, core: (0, j)
    whole = lambda j, core: (0, 0)
    return call(
        unpack_kernel,
        "unpack",
        nbytes=8 * 2**20,
        grid_spec=pltpu.PrefetchScalarGridSpec(
            num_scalar_prefetch=1,
            grid=(STEPS,),
            in_specs=[
                pl.BlockSpec(block, lambda j, core: (jnp.clip(j - 2 * core[0], 0, 1), 0, 0)),
                pl.BlockSpec(block, lambda j, core: (jnp.clip(j - 2 * (1 - core[0]), 0, 1), 0, 0)),
            ],
            out_specs=[
                pl.BlockSpec((H, CHUNK), cols),
                pl.BlockSpec((GB_IN, CHUNK), cols),
                pl.BlockSpec((1, CHUNK), cols),
                pl.BlockSpec((1, GB_IN), whole),
                pl.BlockSpec((1, 1), whole),
            ],
        ),
        out_shape=[
            jax.ShapeDtypeStruct((H, H), f32),
            jax.ShapeDtypeStruct((GB_IN, H), f32),
            jax.ShapeDtypeStruct((1, H), f32),
            jax.ShapeDtypeStruct((1, GB_IN), f32),
            jax.ShapeDtypeStruct((1, 1), f32),
        ],
    )(core, mine, got)


def final_kernel(side, own, same, swp, diag, both):
    j = pl.program_id(0)

    @pl.when(j == 0)
    def _():
        both[0] = (own[...] + same[...].astype(f32)).astype(bf16)

    @pl.when(j == 1)
    def _():
        both[0] = (swp[...].astype(f32) + diag[...].astype(f32)).astype(bf16)


def final_latents(side, own, same, swp, diag):
    n = own.shape[0]
    whole = lambda j, side: (0, 0)
    block = pl.BlockSpec((n, H), whole)
    return call(
        final_kernel,
        "final_latents",
        nbytes=5 * 2**20,
        grid_spec=pltpu.PrefetchScalarGridSpec(
            num_scalar_prefetch=1,
            grid=(2,),
            in_specs=[block] * 4,
            out_specs=pl.BlockSpec(
                (1, n, H), lambda j, side: (jnp.where(j == 0, side[0], 1 - side[0]), 0, 0)
            ),
        ),
        out_shape=jax.ShapeDtypeStruct((2, n, H), bf16),
    )(side, own, same, swp, diag)


def body(latent, edge_src, counts, targets, area, var_weight, w_in, b_in, w_out, b_out):
    l_tile = latent.shape[1]
    g_tile, k_edges = edge_src.shape
    n_vars = w_out.shape[1]
    h = lax.axis_index("xh")
    core = lax.axis_index("c")
    pair = lax.axis_index(("z", "y"))
    tile = 2 * pair + h
    quarter = lax.axis_index(ENS)
    pts = g_tile // 4
    side = jnp.reshape(h, (1,)).astype(jnp.int32)
    core = jnp.reshape(core, (1,)).astype(jnp.int32)
    group = lax.rem(lax.axis_index(PLANE), ROW_GROUPS)
    group = jnp.reshape(group, (1,)).astype(jnp.int32)

    own = lax.dynamic_index_in_dim(latent, h, 0, keepdims=False)
    oth = lax.dynamic_index_in_dim(latent, 1 - h, 0, keepdims=False)
    edges_there = lax.ppermute(edge_src, GRID, SWAP)
    swapped = lax.ppermute(oth, GRID, SWAP)
    diag = lax.ppermute(oth, GRID, DIAG)
    same = lax.ppermute(own, GRID, SAME)

    edges = jnp.where(
        h == 0,
        jnp.concatenate([edge_src, edges_there], axis=0),
        jnp.concatenate([edges_there, edge_src], axis=0),
    )
    step = edges // l_tile - 2 * pair
    block = jnp.mod(jnp.where(h == 0, step, 1 - step), 4)
    local = block * l_tile + jnp.mod(edges, l_tile)
    nodes = lax.broadcasted_iota(jnp.int32, (2 * g_tile, 4 * l_tile), 1)
    nodes_t = lax.broadcasted_iota(jnp.int32, (4 * l_tile, 2 * g_tile), 0)
    pick = jnp.zeros((2 * g_tile, 4 * l_tile), f32)
    pick_t = jnp.zeros((4 * l_tile, 2 * g_tile), f32)
    for k in range(k_edges):
        pick = pick + (local[:, k : k + 1] == nodes).astype(f32)
        pick_t = pick_t + (local[:, k][None, :] == nodes_t).astype(f32)
    pick = pick.astype(bf16)
    pick_t = pick_t.astype(bf16)

    start = quarter * pts
    point = start + jnp.arange(pts, dtype=jnp.int32)
    valid = (point < counts[tile]).astype(f32)
    pad = LANES - n_vars
    var_weight = jnp.pad(var_weight, (0, pad))
    wgt = (lax.dynamic_slice_in_dim(area, start, pts, 0) * valid)[:, None] * var_weight[None, :]
    aim = jnp.pad(lax.dynamic_slice_in_dim(targets, start, pts, 1).T, ((0, 0), (0, pad)))
    w_out_p = jnp.pad(w_out, ((0, 0), (0, pad)))
    b_out_p = jnp.pad(b_out, (0, pad))[None]

    pick, pick_t, aim, wgt = lax.optimization_barrier((pick, pick_t, aim, wgt))
    feats_t, hidden, slope, pred = forward(
        pick, own, swapped, same, diag, w_in, b_in[None], w_out_p, b_out_p
    )
    pred = a2a(pred, GROUP)
    dpred, small = crps(pred, aim, wgt)
    dpred = a2a(dpred, GROUP).reshape(MEMBERS * pts, LANES)
    dpre, send = backward(core, dpred, w_out_p, slope, hidden, feats_t, small)
    got = lax.ppermute(send, "c", [(0, 1), (1, 0)])
    d_own, d_swap, d_same, d_diag = latent_grads(dpre, w_in, pick_t)
    got, d_own = lax.optimization_barrier((got, d_own))
    part = pair_sum(core, dpred, dpre, hidden, feats_t, small, got)
    part = a2a(part, PLANE)
    part, d_swap, d_same, d_diag = lax.optimization_barrier((part, d_swap, d_same, d_diag))
    r_swap = lax.ppermute(d_swap, GRID, back(SWAP))
    r_same = lax.ppermute(d_same, GRID, back(SAME))
    r_diag = lax.ppermute(d_diag, GRID, back(DIAG))
    part = total_and_spread(group, part, 8)
    part = lax.cond(counts[0] >= 0, lambda x: a2a(x, "z"), lambda x: x, part)
    part, r_swap, r_same, r_diag = lax.optimization_barrier((part, r_swap, r_same, r_diag))
    part = total_and_spread(group, part, PARTS)
    part = a2a(part, PLANE)
    got = lax.ppermute(part, "c", [(0, 1), (1, 0)])
    grad_latent = final_latents(side, d_own, r_same, r_swap, r_diag)
    gw_in, gw_out_t, gb_in, gb_out, loss = unpack(core, part, got)
    return (
        grad_latent,
        gw_in,
        gb_in[0],
        gw_out_t.T,
        gb_out[0],
        loss[0, 0],
    )


def solution(mesh):
    fine = Mesh(mesh.devices.reshape(2, 2, 8, 4, 2), ENS + GRID)
    in_specs = (
        P(ENS, GRID, None),
        P(GRID, None),
        P(),
        P(None, GRID),
        P(GRID),
        P(),
        P(),
        P(),
        P(),
        P(),
    )
    out_specs = (P(ENS, GRID, None), P(), P(), P(), P(), P())
    return jax.shard_map(body, mesh=fine, in_specs=in_specs, out_specs=out_specs, check_vma=False)
```

```python
import jax
import jax.numpy as jnp
from jax import lax
from jax.experimental import pallas as pl
from jax.experimental.pallas import tpu as pltpu
from jax.sharding import Mesh, PartitionSpec as P

smooth_sq = 0.0025
smooth_width = 0.05
bf16 = jnp.bfloat16
f32 = jnp.float32

ENS = ("xl", "c")
GRID = ("z", "y", "xh")
GROUP = ("xh", "xl", "c")
PLANE = ("y", "xh", "xl")
MEMBERS = 8
H = 1024
LANES = 128
CHUNK = 256
STEPS = H // CHUNK
ROWS = H + LANES
ROW_GROUPS = 4
PART = ROWS // ROW_GROUPS
PARTS = 16
GB_IN, HIGH, LOW = 100, 101, 102
HIGH_IN_PART = H + HIGH - 3 * PART


def dot(a, b, dims=((1,), (0,))):
    return lax.dot_general(a, b, (dims, ((), ())), preferred_element_type=f32)


def call(kernel, name, flops=0, nbytes=0, trans=0, **kw):
    return pl.pallas_call(
        kernel,
        name=name,
        cost_estimate=pl.CostEstimate(flops=flops, bytes_accessed=nbytes, transcendentals=trans),
        compiler_params=pltpu.CompilerParams(vmem_limit_bytes=24 * 1024 * 1024),
        **kw,
    )


def near(*xs):
    return list(xs)


def pinned(x):
    return pltpu.with_memory_space_constraint(x, pltpu.VMEM)


def far(x):
    return pltpu.with_memory_space_constraint(x, pltpu.HBM)


def out(shape, dtype):
    return jax.ShapeDtypeStruct(shape, dtype)


def ring(shift_odd, shift_even):
    n = 64
    return [(i, (i + (shift_odd if i % 2 else shift_even)) % n) for i in range(n)]


SWAP = ring(-1, 1)
SAME = ring(2, -2)
DIAG = ring(1, -1)


def back(perm):
    return [(b, a) for a, b in perm]


def at(z, y, h):
    return (z % 8 * 4 + y % 4) * 2 + h


PLACES = [(z, y, h) for z in range(8) for y in range(4) for h in range(2)]
BACK_SAME = [(at(z, y, h), at(z, y - 1 if h else y + 1, h)) for z, y, h in PLACES]
BACK_DIAG = [(at(z, y, h), at(z, y + 1 if h else y - 1, 1 - h)) for z, y, h in PLACES]
CARRY = [
    (at(z, y, h), at(z + 1 if y else z - 1, y, h)) for z, y, h in PLACES if y in (0, 3)
]


def a2a(x, axes):
    return lax.all_to_all(x, axes, split_axis=0, concat_axis=0, tiled=True)


def forward_kernel(pick, own, swp, same, diag, w_in, b_in, w_out, b_out, feats_t, hid, slope, pred, w_here, sem):
    n = own.shape[0]
    copy = pltpu.make_async_copy(w_in, w_here, sem)
    copy.start()
    total = dot(pick[:, :n], own[...])
    for k, ref in enumerate((swp, same, diag)):
        total = total + dot(pick[:, (k + 1) * n : (k + 2) * n], ref[...])
    feats = (total / 3.0).astype(bf16)
    feats_t[...] = feats.T
    copy.wait()
    v = dot(feats, w_here[...]) + b_in[...]
    cdf = 0.5 * (1.0 + lax.erf(v * 0.7071067811865476))
    slope[...] = (cdf + v * jnp.exp(-0.5 * v * v) * 0.3989422804014327).astype(bf16)
    h = (v * cdf).astype(bf16)
    hid[...] = h
    p = dot(h, w_out[...]) + b_out[...]
    pts = pred.shape[1]
    for i in range(MEMBERS):
        pred[i] = p[i * pts : (i + 1) * pts]


def forward(pick, own, swp, same, diag, w_in, b_in, w_out, b_out):
    m = pick.shape[0]
    return call(
        forward_kernel,
        "forward",
        flops=2 * m * H * (2 * H + LANES),
        nbytes=12 * 2**20,
        trans=2 * m * H,
        in_specs=[pl.BlockSpec(memory_space=pltpu.VMEM)] * 5
        + [pl.BlockSpec(memory_space=pl.ANY)]
        + [pl.BlockSpec(memory_space=pltpu.VMEM)] * 3,
        scratch_shapes=[pltpu.VMEM((H, H), bf16), pltpu.SemaphoreType.DMA],
        out_shape=[
            out((H, m), bf16),
            out((m, H), bf16),
            out((m, H), bf16),
            jax.ShapeDtypeStruct((MEMBERS, m // MEMBERS, LANES), f32),
        ],
    )(*near(pick, own, swp, same, diag), far(w_in), *near(b_in, w_out, b_out))


def crps_kernel(pred, aim, wgt, dpred, small):
    mm = float(MEMBERS)
    pts = pred.shape[1]
    gb = jnp.zeros((1, LANES), f32)
    loss = jnp.zeros((1, LANES), f32)
    for r in range(0, pts, 16):
        p = [pred[i, r : r + 16, :] for i in range(MEMBERS)]
        pair = [jnp.zeros((16, LANES), f32) for _ in range(MEMBERS)]
        gaps = jnp.zeros((16, LANES), f32)
        hits = jnp.zeros((16, LANES), f32)
        for i in range(MEMBERS):
            for j in range(i + 1, MEMBERS):
                d = p[i] - p[j]
                sq = d * d + smooth_sq
                inv = lax.rsqrt(sq)
                gaps = gaps + (sq * inv - smooth_width)
                pair[i] = pair[i] + d * inv
                pair[j] = pair[j] - d * inv
        w = wgt[r : r + 16, :]
        t = aim[r : r + 16, :]
        g_sum = jnp.zeros((16, LANES), f32)
        for i in range(MEMBERS):
            d = p[i] - t
            sq = d * d + smooth_sq
            inv = lax.rsqrt(sq)
            hits = hits + (sq * inv - smooth_width)
            g = w * (d * inv / mm - pair[i] / (mm * (mm - 1.0)))
            g_sum = g_sum + g
            dpred[i, r : r + 16, :] = g.astype(bf16)
        gb = gb + jnp.sum(g_sum, axis=0, keepdims=True)
        loss = loss + jnp.sum(w * (hits / mm - gaps / (mm * (mm - 1.0))), axis=0, keepdims=True)
    small[:, :LANES] = gb
    small[:, LANES:] = loss


def crps(pred, aim, wgt):
    pts = aim.shape[0]
    return call(
        crps_kernel,
        "crps",
        flops=40 * 36 * pts * LANES,
        nbytes=2**19,
        trans=36 * pts * LANES,
        out_shape=[
            jax.ShapeDtypeStruct((MEMBERS, pts, LANES), bf16),
            out((1, 2 * LANES), f32),
        ],
    )(*near(pred, aim, wgt))


def packed(half, feats_t, dpre, dpred, hid, small):
    cols = pl.ds(pl.multiple_of(half * (H // 2), H // 2), H // 2)
    d = dpre[:, cols]
    gb_in = jnp.sum(d.astype(f32), axis=0, keepdims=True)
    foot = dot(dpred[...], hid[:, cols], ((0,), (0,)))
    row = lax.broadcasted_iota(jnp.int32, foot.shape, 0)
    s = jnp.concatenate([small[...], jnp.zeros_like(small[...])], axis=1)
    s = jnp.where(half == 0, s, 0.0)
    high = s.astype(bf16).astype(f32)
    foot = jnp.where(row == GB_IN, gb_in, foot)
    foot = jnp.where(row == HIGH, high, foot)
    foot = jnp.where(row == LOW, s - high, foot)
    main = dot(feats_t[...], d)
    for g in range(ROW_GROUPS):
        lanes = slice(g * LANES, (g + 1) * LANES)
        for r in range(ROW_GROUPS):
            block = main[r * PART : (r + 1) * PART, lanes]
            if r == ROW_GROUPS - 1:
                block = jnp.concatenate([block, foot[:, lanes]], axis=0)
            yield g * ROW_GROUPS + r, block


def backward_kernel(core, dpred, w_out, slope, hid, feats_t, small, dpre, send):
    d = dot(dpred[...], w_out[...], ((1,), (1,))) * slope[...].astype(f32)
    dpre[...] = d.astype(bf16)
    for i, block in packed(1 - core[0], feats_t, dpre, dpred, hid, small):
        send[i] = block.astype(bf16)


def backward(core, dpred, w_out, slope, hid, feats_t, small):
    m = dpred.shape[0]
    return call(
        backward_kernel,
        "backward",
        flops=m * H * (H + 4 * LANES),
        nbytes=6 * 2**20,
        in_specs=[pl.BlockSpec(memory_space=pltpu.SMEM)]
        + [pl.BlockSpec(memory_space=pltpu.VMEM)] * 6,
        out_shape=[out((m, H), bf16), out((PARTS, PART, LANES), bf16)],
    )(core, *near(dpred, w_out, slope, hid, feats_t, small))


def latent_kernel(dpre, w_in, pick_t, own, swp, same, diag):
    d = (dot(dpre[...], w_in[...], ((1,), (1,))) / 3.0).astype(bf16)
    n = own.shape[0]
    for k, ref in enumerate((own, swp, same, diag)):
        ref[...] = dot(pick_t[k * n : (k + 1) * n, :], d).astype(ref.dtype)


def latent_grads(dpre, w_in, pick_t):
    m = dpre.shape[0]
    n = pick_t.shape[0] // 4
    return call(
        latent_kernel,
        "latent_grads",
        flops=4 * m * H * H,
        nbytes=8 * 2**20,
        out_shape=[out((n, H), f32)] + [jax.ShapeDtypeStruct((n, H), bf16)] * 3,
    )(*near(dpre, w_in, pick_t))


def resplit(total):
    row = lax.broadcasted_iota(jnp.int32, total.shape, 0)
    both = total[HIGH_IN_PART : HIGH_IN_PART + 1] + total[HIGH_IN_PART + 1 : HIGH_IN_PART + 2]
    high = both.astype(bf16).astype(f32)
    total_high = jnp.where(row == HIGH_IN_PART, high, total)
    return jnp.where(row == HIGH_IN_PART + 1, both - high, total_high).astype(bf16)


def pair_kernel(core, dpred, dpre, hid, feats_t, small, got, part):
    for i, block in packed(core[0], feats_t, dpre, dpred, hid, small):
        total = block + got[i].astype(f32)
        if i % ROW_GROUPS == ROW_GROUPS - 1:
            total = resplit(total)
        part[i] = total.astype(bf16)


def pair_sum(core, dpred, dpre, hid, feats_t, small, got):
    m = dpred.shape[0]
    return call(
        pair_kernel,
        "pair_sum",
        flops=m * H * (H + 2 * LANES),
        nbytes=6 * 2**20,
        in_specs=[pl.BlockSpec(memory_space=pltpu.SMEM)]
        + [pl.BlockSpec(memory_space=pltpu.VMEM)] * 6,
        out_shape=jax.ShapeDtypeStruct(got.shape, bf16),
    )(core, *near(dpred, dpre, hid, feats_t, small, got))


def total_kernel(group, parts, copies):
    total = parts[0].astype(f32)
    for i in range(1, parts.shape[0]):
        total = total + parts[i].astype(f32)
    last = group[0] == ROW_GROUPS - 1
    done = jnp.where(last, resplit(total).astype(f32), total).astype(bf16)
    for i in range(copies.shape[0]):
        copies[i] = done


def total_and_spread(group, parts, copies):
    n = parts.shape[0]
    return call(
        total_kernel,
        "total",
        flops=n * PART * LANES,
        nbytes=2 * (n + copies) * PART * LANES,
        in_specs=[
            pl.BlockSpec(memory_space=pltpu.SMEM),
            pl.BlockSpec(memory_space=pltpu.VMEM),
        ],
        out_shape=jax.ShapeDtypeStruct((copies, PART, LANES), bf16),
    )(group, pinned(parts))


def unpack_kernel(core, mine, got, gw_in, gw_out_t, gb_in, gb_out, loss):
    j = pl.program_id(0)

    def put(ref):
        for g in range(2):
            lanes = slice(g * LANES, (g + 1) * LANES)
            base = g * ROW_GROUPS
            for r in range(ROW_GROUPS - 1):
                gw_in[r * PART : (r + 1) * PART, lanes] = ref[base + r].astype(f32)
            r = ROW_GROUPS - 1
            gw_in[r * PART :, lanes] = ref[base + r, : H - r * PART, :].astype(f32)
            foot = ref[base + r, H - r * PART :, :].astype(f32)
            gw_out_t[:, lanes] = foot[:GB_IN]
            gb_in[:, lanes] = foot[GB_IN : GB_IN + 1]
            small = foot[HIGH : HIGH + 1] + foot[LOW : LOW + 1]

            @pl.when(j == 0)
            def _():
                if g == 0:
                    gb_out[...] = small[:, :GB_IN]
                else:
                    loss[...] = jnp.sum(small, axis=1, keepdims=True)

    here = j // 2 == core[0]

    @pl.when(here)
    def _():
        put(mine)

    @pl.when(jnp.logical_not(here))
    def _():
        put(got)


def unpack(core, mine, got):
    block = (2 * ROW_GROUPS, PART, LANES)
    cols = lambda j, core: (0, j)
    whole = lambda j, core: (0, 0)
    return call(
        unpack_kernel,
        "unpack",
        nbytes=8 * 2**20,
        grid_spec=pltpu.PrefetchScalarGridSpec(
            num_scalar_prefetch=1,
            grid=(STEPS,),
            in_specs=[
                pl.BlockSpec(block, lambda j, core: (jnp.clip(j - 2 * core[0], 0, 1), 0, 0)),
                pl.BlockSpec(block, lambda j, core: (jnp.clip(j - 2 * (1 - core[0]), 0, 1), 0, 0)),
            ],
            out_specs=[
                pl.BlockSpec((H, CHUNK), cols),
                pl.BlockSpec((GB_IN, CHUNK), cols),
                pl.BlockSpec((1, CHUNK), cols),
                pl.BlockSpec((1, GB_IN), whole),
                pl.BlockSpec((1, 1), whole),
            ],
        ),
        out_shape=[
            jax.ShapeDtypeStruct((H, H), f32),
            jax.ShapeDtypeStruct((GB_IN, H), f32),
            jax.ShapeDtypeStruct((1, H), f32),
            jax.ShapeDtypeStruct((1, GB_IN), f32),
            jax.ShapeDtypeStruct((1, 1), f32),
        ],
    )(core, pinned(mine), pinned(got))


def final_kernel(side, own, same, swp, diag, both):
    j = pl.program_id(0)

    @pl.when(j == 0)
    def _():
        both[0] = (own[...] + same[...].astype(f32)).astype(bf16)

    @pl.when(j == 1)
    def _():
        both[0] = (swp[...].astype(f32) + diag[...].astype(f32)).astype(bf16)


def final_latents(side, own, same, swp, diag):
    n = own.shape[0]
    whole = lambda j, side: (0, 0)
    block = pl.BlockSpec((n, H), whole)
    return call(
        final_kernel,
        "final_latents",
        nbytes=5 * 2**20,
        grid_spec=pltpu.PrefetchScalarGridSpec(
            num_scalar_prefetch=1,
            grid=(2,),
            in_specs=[block] * 4,
            out_specs=pl.BlockSpec(
                (1, n, H), lambda j, side: (jnp.where(j == 0, side[0], 1 - side[0]), 0, 0)
            ),
        ),
        out_shape=jax.ShapeDtypeStruct((2, n, H), bf16),
    )(side, own, same, swp, diag)


def body(latent, edge_src, counts, targets, area, var_weight, w_in, b_in, w_out, b_out):
    l_tile = latent.shape[1]
    g_tile, k_edges = edge_src.shape
    n_vars = w_out.shape[1]
    h = lax.axis_index("xh")
    core = lax.axis_index("c")
    pair = lax.axis_index(("z", "y"))
    tile = 2 * pair + h
    quarter = lax.axis_index(ENS)
    pts = g_tile // 4
    side = jnp.reshape(h, (1,)).astype(jnp.int32)
    core = jnp.reshape(core, (1,)).astype(jnp.int32)
    group = lax.rem(lax.axis_index(PLANE), ROW_GROUPS)
    group = jnp.reshape(group, (1,)).astype(jnp.int32)

    own = lax.dynamic_index_in_dim(latent, h, 0, keepdims=False)
    oth = lax.dynamic_index_in_dim(latent, 1 - h, 0, keepdims=False)
    edges_there = lax.ppermute(edge_src, GRID, SWAP)
    swapped = lax.ppermute(oth, GRID, SWAP)
    diag = lax.ppermute(oth, GRID, DIAG)
    same = lax.ppermute(own, GRID, SAME)

    edges = jnp.where(
        h == 0,
        jnp.concatenate([edge_src, edges_there], axis=0),
        jnp.concatenate([edges_there, edge_src], axis=0),
    )
    step = edges // l_tile - 2 * pair
    block = jnp.mod(jnp.where(h == 0, step, 1 - step), 4)
    local = block * l_tile + jnp.mod(edges, l_tile)
    nodes = lax.broadcasted_iota(jnp.int32, (2 * g_tile, 4 * l_tile), 1)
    nodes_t = lax.broadcasted_iota(jnp.int32, (4 * l_tile, 2 * g_tile), 0)
    pick = jnp.zeros((2 * g_tile, 4 * l_tile), f32)
    pick_t = jnp.zeros((4 * l_tile, 2 * g_tile), f32)
    for k in range(k_edges):
        pick = pick + (local[:, k : k + 1] == nodes).astype(f32)
        pick_t = pick_t + (local[:, k][None, :] == nodes_t).astype(f32)
    pick = pick.astype(bf16)
    pick_t = pick_t.astype(bf16)

    start = quarter * pts
    point = start + jnp.arange(pts, dtype=jnp.int32)
    valid = (point < counts[tile]).astype(f32)
    pad = LANES - n_vars
    var_weight = jnp.pad(var_weight, (0, pad))
    wgt = (lax.dynamic_slice_in_dim(area, start, pts, 0) * valid)[:, None] * var_weight[None, :]
    aim = jnp.pad(lax.dynamic_slice_in_dim(targets, start, pts, 1).T, ((0, 0), (0, pad)))
    w_out_p = jnp.pad(w_out, ((0, 0), (0, pad)))
    b_out_p = jnp.pad(b_out, (0, pad))[None]

    pick, pick_t, aim, wgt = lax.optimization_barrier((pick, pick_t, aim, wgt))
    feats_t, hidden, slope, pred = forward(
        pick, own, swapped, same, diag, w_in, b_in[None], w_out_p, b_out_p
    )
    pred = a2a(pred, GROUP)
    dpred, small = crps(pred, aim, wgt)
    dpred = a2a(dpred, GROUP).reshape(MEMBERS * pts, LANES)
    dpre, send = backward(core, dpred, w_out_p, slope, hidden, feats_t, small)
    got = lax.ppermute(send, "c", [(0, 1), (1, 0)])
    d_own, d_swap, d_same, d_diag = latent_grads(dpre, w_in, pick_t)
    got, d_own = lax.optimization_barrier((got, d_own))
    part = pair_sum(core, dpred, dpre, hidden, feats_t, small, got)
    y = lax.axis_index("y")
    up, down = jnp.logical_and(y == 3, h == 0), jnp.logical_and(y == 0, h == 1)
    same_crosses = jnp.logical_or(up, down)
    up, down = jnp.logical_and(y == 3, h == 1), jnp.logical_and(y == 0, h == 0)
    diag_crosses = jnp.logical_or(up, down)
    crossed = lax.ppermute(jnp.where(same_crosses, d_same, d_diag), GRID, CARRY)
    d_same = jnp.where(same_crosses, crossed, d_same)
    d_diag = jnp.where(diag_crosses, crossed, d_diag)
    part = a2a(part, PLANE)
    part, d_swap, d_same, d_diag = lax.optimization_barrier((part, d_swap, d_same, d_diag))
    r_swap = lax.ppermute(d_swap, GRID, back(SWAP))
    r_same = lax.ppermute(d_same, GRID, BACK_SAME)
    r_diag = lax.ppermute(d_diag, GRID, BACK_DIAG)
    def planes(x):
        x = a2a(total_and_spread(group, x, 8), "z")
        return a2a(total_and_spread(group, x, PARTS), PLANE)

    part = lax.cond(counts[0] >= 0, planes, lambda x: x, part)
    part, r_swap, r_same, r_diag = lax.optimization_barrier((part, r_swap, r_same, r_diag))
    got = lax.ppermute(part, "c", [(0, 1), (1, 0)])
    grad_latent = final_latents(side, d_own, r_same, r_swap, r_diag)
    gw_in, gw_out_t, gb_in, gb_out, loss = unpack(core, part, got)
    return (
        grad_latent,
        gw_in,
        gb_in[0],
        gw_out_t.T,
        gb_out[0],
        loss[0, 0],
    )


def solution(mesh):
    fine = Mesh(mesh.devices.reshape(2, 2, 8, 4, 2), ENS + GRID)
    in_specs = (
        P(ENS, GRID, None),
        P(GRID, None),
        P(),
        P(None, GRID),
        P(GRID),
        P(),
        P(),
        P(),
        P(),
        P(),
    )
    out_specs = (P(ENS, GRID, None), P(), P(), P(), P(), P())
    return jax.shard_map(body, mesh=fine, in_specs=in_specs, out_specs=out_specs, check_vma=False)
```

```python
import jax
import jax.numpy as jnp
from jax import lax
from jax.experimental import pallas as pl
from jax.experimental.pallas import tpu as pltpu
from jax.sharding import Mesh, PartitionSpec as P

smooth_sq = 0.0025
smooth_width = 0.05
bf16 = jnp.bfloat16
f32 = jnp.float32

ENS = ("xl", "c")
GRID = ("z", "y", "xh")
GROUP = ("xh", "xl", "c")
PLANE = ("y", "xh", "xl")
MEMBERS = 8
H = 1024
LANES = 128
CHUNK = 256
STEPS = H // CHUNK
ROWS = H + LANES
ROW_GROUPS = 4
PART = ROWS // ROW_GROUPS
PARTS = 16
GB_IN, HIGH, LOW = 100, 101, 102
HIGH_IN_PART = H + HIGH - 3 * PART


def dot(a, b, dims=((1,), (0,))):
    return lax.dot_general(a, b, (dims, ((), ())), preferred_element_type=f32)


def call(kernel, name, flops=0, nbytes=0, trans=0, **kw):
    return pl.pallas_call(
        kernel,
        name=name,
        cost_estimate=pl.CostEstimate(flops=flops, bytes_accessed=nbytes, transcendentals=trans),
        compiler_params=pltpu.CompilerParams(vmem_limit_bytes=24 * 1024 * 1024),
        **kw,
    )


def near(*xs):
    return list(xs)


def pinned(x):
    return pltpu.with_memory_space_constraint(x, pltpu.VMEM)


def far(x):
    return pltpu.with_memory_space_constraint(x, pltpu.HBM)


def out(shape, dtype):
    return jax.ShapeDtypeStruct(shape, dtype)


def ring(shift_odd, shift_even):
    n = 64
    return [(i, (i + (shift_odd if i % 2 else shift_even)) % n) for i in range(n)]


SWAP = ring(-1, 1)
SAME = ring(2, -2)
DIAG = ring(1, -1)


def back(perm):
    return [(b, a) for a, b in perm]


def at(z, y, h):
    return (z % 8 * 4 + y % 4) * 2 + h


PLACES = [(z, y, h) for z in range(8) for y in range(4) for h in range(2)]
BACK_SAME = [(at(z, y, h), at(z, y - 1 if h else y + 1, h)) for z, y, h in PLACES]
BACK_DIAG = [(at(z, y, h), at(z, y + 1 if h else y - 1, 1 - h)) for z, y, h in PLACES]
CARRY = [
    (at(z, y, h), at(z + 1 if y else z - 1, y, h)) for z, y, h in PLACES if y in (0, 3)
]


def a2a(x, axes):
    return lax.all_to_all(x, axes, split_axis=0, concat_axis=0, tiled=True)


def forward_kernel(pick, own, swp, same, diag, w_in, b_in, w_out, b_out, feats_t, hid, slope, pred, w_here, sem):
    n = own.shape[0]
    copy = pltpu.make_async_copy(w_in, w_here, sem)
    copy.start()
    total = dot(pick[:, :n], own[...])
    for k, ref in enumerate((swp, same, diag)):
        total = total + dot(pick[:, (k + 1) * n : (k + 2) * n], ref[...])
    feats = (total / 3.0).astype(bf16)
    feats_t[...] = feats.T
    copy.wait()
    v = dot(feats, w_here[...]) + b_in[...]
    cdf = 0.5 * (1.0 + lax.erf(v * 0.7071067811865476))
    slope[...] = (cdf + v * jnp.exp(-0.5 * v * v) * 0.3989422804014327).astype(bf16)
    h = (v * cdf).astype(bf16)
    hid[...] = h
    p = dot(h, w_out[...]) + b_out[...]
    pts = pred.shape[1]
    for i in range(MEMBERS):
        pred[i] = p[i * pts : (i + 1) * pts]


def forward(pick, own, swp, same, diag, w_in, b_in, w_out, b_out):
    m = pick.shape[0]
    return call(
        forward_kernel,
        "forward",
        flops=2 * m * H * (2 * H + LANES),
        nbytes=12 * 2**20,
        trans=2 * m * H,
        in_specs=[pl.BlockSpec(memory_space=pltpu.VMEM)] * 5
        + [pl.BlockSpec(memory_space=pl.ANY)]
        + [pl.BlockSpec(memory_space=pltpu.VMEM)] * 3,
        scratch_shapes=[pltpu.VMEM((H, H), bf16), pltpu.SemaphoreType.DMA],
        out_shape=[
            out((H, m), bf16),
            out((m, H), bf16),
            out((m, H), bf16),
            jax.ShapeDtypeStruct((MEMBERS, m // MEMBERS, LANES), f32),
        ],
    )(*near(pick, own, swp, same, diag), far(w_in), *near(b_in, w_out, b_out))


def crps_kernel(pred, aim, wgt, dpred, small):
    mm = float(MEMBERS)
    pts = pred.shape[1]
    gb = jnp.zeros((1, LANES), f32)
    loss = jnp.zeros((1, LANES), f32)
    for r in range(0, pts, 16):
        p = [pred[i, r : r + 16, :] for i in range(MEMBERS)]
        pair = [jnp.zeros((16, LANES), f32) for _ in range(MEMBERS)]
        gaps = jnp.zeros((16, LANES), f32)
        hits = jnp.zeros((16, LANES), f32)
        for i in range(MEMBERS):
            for j in range(i + 1, MEMBERS):
                d = p[i] - p[j]
                sq = d * d + smooth_sq
                inv = lax.rsqrt(sq)
                gaps = gaps + (sq * inv - smooth_width)
                pair[i] = pair[i] + d * inv
                pair[j] = pair[j] - d * inv
        w = wgt[r : r + 16, :]
        t = aim[r : r + 16, :]
        g_sum = jnp.zeros((16, LANES), f32)
        for i in range(MEMBERS):
            d = p[i] - t
            sq = d * d + smooth_sq
            inv = lax.rsqrt(sq)
            hits = hits + (sq * inv - smooth_width)
            g = w * (d * inv / mm - pair[i] / (mm * (mm - 1.0)))
            g_sum = g_sum + g
            dpred[i, r : r + 16, :] = g.astype(bf16)
        gb = gb + jnp.sum(g_sum, axis=0, keepdims=True)
        loss = loss + jnp.sum(w * (hits / mm - gaps / (mm * (mm - 1.0))), axis=0, keepdims=True)
    small[:, :LANES] = gb
    small[:, LANES:] = loss


def crps(pred, aim, wgt):
    pts = aim.shape[0]
    return call(
        crps_kernel,
        "crps",
        flops=40 * 36 * pts * LANES,
        nbytes=2**19,
        trans=36 * pts * LANES,
        out_shape=[
            jax.ShapeDtypeStruct((MEMBERS, pts, LANES), bf16),
            out((1, 2 * LANES), f32),
        ],
    )(*near(pred, aim, wgt))


def packed(half, feats_t, dpre, dpred, hid, small):
    cols = pl.ds(pl.multiple_of(half * (H // 2), H // 2), H // 2)
    d = dpre[:, cols]
    gb_in = jnp.sum(d.astype(f32), axis=0, keepdims=True)
    foot = dot(dpred[...], hid[:, cols], ((0,), (0,)))
    row = lax.broadcasted_iota(jnp.int32, foot.shape, 0)
    s = jnp.concatenate([small[...], jnp.zeros_like(small[...])], axis=1)
    s = jnp.where(half == 0, s, 0.0)
    high = s.astype(bf16).astype(f32)
    foot = jnp.where(row == GB_IN, gb_in, foot)
    foot = jnp.where(row == HIGH, high, foot)
    foot = jnp.where(row == LOW, s - high, foot)
    main = dot(feats_t[...], d)
    for g in range(ROW_GROUPS):
        lanes = slice(g * LANES, (g + 1) * LANES)
        for r in range(ROW_GROUPS):
            block = main[r * PART : (r + 1) * PART, lanes]
            if r == ROW_GROUPS - 1:
                block = jnp.concatenate([block, foot[:, lanes]], axis=0)
            yield g * ROW_GROUPS + r, block


def backward_kernel(core, dpred, w_out, slope, hid, feats_t, small, dpre, send):
    d = dot(dpred[...], w_out[...], ((1,), (1,))) * slope[...].astype(f32)
    dpre[...] = d.astype(bf16)
    for i, block in packed(1 - core[0], feats_t, dpre, dpred, hid, small):
        send[i] = block.astype(bf16)


def backward(core, dpred, w_out, slope, hid, feats_t, small):
    m = dpred.shape[0]
    return call(
        backward_kernel,
        "backward",
        flops=m * H * (H + 4 * LANES),
        nbytes=6 * 2**20,
        in_specs=[pl.BlockSpec(memory_space=pltpu.SMEM)]
        + [pl.BlockSpec(memory_space=pltpu.VMEM)] * 6,
        out_shape=[out((m, H), bf16), out((PARTS, PART, LANES), bf16)],
    )(core, *near(dpred, w_out, slope, hid, feats_t, small))


def latent_kernel(dpre, w_in, pick_t, own, swp, same, diag):
    d = (dot(dpre[...], w_in[...], ((1,), (1,))) / 3.0).astype(bf16)
    n = own.shape[0]
    for k, ref in enumerate((own, swp, same, diag)):
        ref[...] = dot(pick_t[k * n : (k + 1) * n, :], d).astype(ref.dtype)


def latent_grads(dpre, w_in, pick_t):
    m = dpre.shape[0]
    n = pick_t.shape[0] // 4
    return call(
        latent_kernel,
        "latent_grads",
        flops=4 * m * H * H,
        nbytes=8 * 2**20,
        out_shape=[pltpu.HBM((n, H), f32)] + [pltpu.HBM((n, H), bf16)] * 3,
    )(*near(dpre, w_in, pick_t))


def resplit(total):
    row = lax.broadcasted_iota(jnp.int32, total.shape, 0)
    both = total[HIGH_IN_PART : HIGH_IN_PART + 1] + total[HIGH_IN_PART + 1 : HIGH_IN_PART + 2]
    high = both.astype(bf16).astype(f32)
    total_high = jnp.where(row == HIGH_IN_PART, high, total)
    return jnp.where(row == HIGH_IN_PART + 1, both - high, total_high).astype(bf16)


def pair_kernel(core, dpred, dpre, hid, feats_t, small, got, part):
    for i, block in packed(core[0], feats_t, dpre, dpred, hid, small):
        total = block + got[i].astype(f32)
        if i % ROW_GROUPS == ROW_GROUPS - 1:
            total = resplit(total)
        part[i] = total.astype(bf16)


def pair_sum(core, dpred, dpre, hid, feats_t, small, got):
    m = dpred.shape[0]
    return call(
        pair_kernel,
        "pair_sum",
        flops=m * H * (H + 2 * LANES),
        nbytes=6 * 2**20,
        in_specs=[pl.BlockSpec(memory_space=pltpu.SMEM)]
        + [pl.BlockSpec(memory_space=pltpu.VMEM)] * 6,
        out_shape=jax.ShapeDtypeStruct(got.shape, bf16),
    )(core, *near(dpred, dpre, hid, feats_t, small, got))


def total_kernel(group, parts, copies):
    total = parts[0].astype(f32)
    for i in range(1, parts.shape[0]):
        total = total + parts[i].astype(f32)
    last = group[0] == ROW_GROUPS - 1
    done = jnp.where(last, resplit(total).astype(f32), total).astype(bf16)
    for i in range(copies.shape[0]):
        copies[i] = done


def total_and_spread(group, parts, copies):
    n = parts.shape[0]
    return call(
        total_kernel,
        "total",
        flops=n * PART * LANES,
        nbytes=2 * (n + copies) * PART * LANES,
        in_specs=[
            pl.BlockSpec(memory_space=pltpu.SMEM),
            pl.BlockSpec(memory_space=pltpu.VMEM),
        ],
        out_shape=jax.ShapeDtypeStruct((copies, PART, LANES), bf16),
    )(group, pinned(parts))


def unpack_half(half, parts, gw_in, gw_out_t, gb_in, keep):
    j = pl.program_id(0)
    for g in range(2):
        lanes = slice(g * LANES, (g + 1) * LANES)
        base = g * ROW_GROUPS
        for r in range(ROW_GROUPS - 1):
            gw_in[r * PART : (r + 1) * PART, lanes] = parts[base + r].astype(f32)
        r = ROW_GROUPS - 1
        gw_in[r * PART :, lanes] = parts[base + r, : H - r * PART, :].astype(f32)
        foot = parts[base + r, H - r * PART :, :].astype(f32)
        gw_out_t[:, lanes] = foot[:GB_IN]
        gb_in[:, lanes] = foot[GB_IN : GB_IN + 1]
        small = foot[HIGH : HIGH + 1] + foot[LOW : LOW + 1]

        @pl.when(jnp.logical_and(j == 0, half[0] == 0))
        def _():
            keep(g, small)


def first_kernel(half, parts, gw_in, gw_out_t, gb_in, gb_out, loss):
    @pl.when(pl.program_id(0) == 0)
    def _():
        gb_out[...] = jnp.zeros_like(gb_out)
        loss[...] = jnp.zeros_like(loss)

    def keep(g, small):
        if g == 0:
            gb_out[...] = small[:, :GB_IN]
        else:
            loss[...] = jnp.sum(small, axis=1, keepdims=True)

    unpack_half(half, parts, gw_in, gw_out_t, gb_in, keep)


def second_kernel(half, parts, a, b, c, gb_one, loss_one, gw_in, gw_out_t, gb_in, gb_out, loss):
    del a, b, c

    @pl.when(pl.program_id(0) == 0)
    def _():
        gb_out[...] = gb_one[...]
        loss[...] = loss_one[...]

    def keep(g, small):
        if g == 0:
            gb_out[...] = small[:, :GB_IN]
        else:
            loss[...] = jnp.sum(small, axis=1, keepdims=True)

    unpack_half(half, parts, gw_in, gw_out_t, gb_in, keep)


def unpack(half, parts, first=None):
    cols = lambda j, half: (0, 2 * half[0] + j)
    whole = lambda j, half: (0, 0)
    anywhere = pl.BlockSpec(memory_space=pl.ANY)
    smalls = [pl.BlockSpec((1, GB_IN), whole), pl.BlockSpec((1, 1), whole)]
    more = [] if first is None else [anywhere] * 3 + smalls
    return call(
        first_kernel if first is None else second_kernel,
        "unpack_first" if first is None else "unpack_second",
        nbytes=4 * 2**20,
        grid_spec=pltpu.PrefetchScalarGridSpec(
            num_scalar_prefetch=1,
            grid=(2,),
            in_specs=[
                pl.BlockSpec((2 * ROW_GROUPS, PART, LANES), lambda j, half: (j, 0, 0)),
            ]
            + more,
            out_specs=[
                pl.BlockSpec((H, CHUNK), cols),
                pl.BlockSpec((GB_IN, CHUNK), cols),
                pl.BlockSpec((1, CHUNK), cols),
            ]
            + smalls,
        ),
        out_shape=[
            jax.ShapeDtypeStruct((H, H), f32),
            jax.ShapeDtypeStruct((GB_IN, H), f32),
            jax.ShapeDtypeStruct((1, H), f32),
            jax.ShapeDtypeStruct((1, GB_IN), f32),
            jax.ShapeDtypeStruct((1, 1), f32),
        ],
        input_output_aliases={} if first is None else {2: 0, 3: 1, 4: 2},
    )(half, parts, *([] if first is None else first))


def final_kernel(side, own, same, swp, diag, both):
    j = pl.program_id(0)

    @pl.when(j == 0)
    def _():
        both[0] = (own[...] + same[...].astype(f32)).astype(bf16)

    @pl.when(j == 1)
    def _():
        both[0] = (swp[...].astype(f32) + diag[...].astype(f32)).astype(bf16)


def final_latents(side, own, same, swp, diag):
    n = own.shape[0]
    whole = lambda j, side: (0, 0)
    block = pl.BlockSpec((n, H), whole)
    return call(
        final_kernel,
        "final_latents",
        nbytes=5 * 2**20,
        grid_spec=pltpu.PrefetchScalarGridSpec(
            num_scalar_prefetch=1,
            grid=(2,),
            in_specs=[block] * 4,
            out_specs=pl.BlockSpec(
                (1, n, H), lambda j, side: (jnp.where(j == 0, side[0], 1 - side[0]), 0, 0)
            ),
        ),
        out_shape=jax.ShapeDtypeStruct((2, n, H), bf16),
    )(side, own, same, swp, diag)


def body(latent, edge_src, counts, targets, area, var_weight, w_in, b_in, w_out, b_out):
    l_tile = latent.shape[1]
    g_tile, k_edges = edge_src.shape
    n_vars = w_out.shape[1]
    h = lax.axis_index("xh")
    core = lax.axis_index("c")
    pair = lax.axis_index(("z", "y"))
    tile = 2 * pair + h
    quarter = lax.axis_index(ENS)
    pts = g_tile // 4
    side = jnp.reshape(h, (1,)).astype(jnp.int32)
    core = jnp.reshape(core, (1,)).astype(jnp.int32)
    group = lax.rem(lax.axis_index(PLANE), ROW_GROUPS)
    group = jnp.reshape(group, (1,)).astype(jnp.int32)

    own = lax.dynamic_index_in_dim(latent, h, 0, keepdims=False)
    oth = lax.dynamic_index_in_dim(latent, 1 - h, 0, keepdims=False)
    edges_there = lax.ppermute(edge_src, GRID, SWAP)
    swapped = lax.ppermute(oth, GRID, SWAP)
    diag = lax.ppermute(oth, GRID, DIAG)
    same = lax.ppermute(own, GRID, SAME)

    edges = jnp.where(
        h == 0,
        jnp.concatenate([edge_src, edges_there], axis=0),
        jnp.concatenate([edges_there, edge_src], axis=0),
    )
    step = edges // l_tile - 2 * pair
    block = jnp.mod(jnp.where(h == 0, step, 1 - step), 4)
    local = block * l_tile + jnp.mod(edges, l_tile)
    nodes = lax.broadcasted_iota(jnp.int32, (2 * g_tile, 4 * l_tile), 1)
    nodes_t = lax.broadcasted_iota(jnp.int32, (4 * l_tile, 2 * g_tile), 0)
    pick = jnp.zeros((2 * g_tile, 4 * l_tile), f32)
    pick_t = jnp.zeros((4 * l_tile, 2 * g_tile), f32)
    for k in range(k_edges):
        pick = pick + (local[:, k : k + 1] == nodes).astype(f32)
        pick_t = pick_t + (local[:, k][None, :] == nodes_t).astype(f32)
    pick = pick.astype(bf16)
    pick_t = pick_t.astype(bf16)

    start = quarter * pts
    point = start + jnp.arange(pts, dtype=jnp.int32)
    valid = (point < counts[tile]).astype(f32)
    pad = LANES - n_vars
    var_weight = jnp.pad(var_weight, (0, pad))
    wgt = (lax.dynamic_slice_in_dim(area, start, pts, 0) * valid)[:, None] * var_weight[None, :]
    aim = jnp.pad(lax.dynamic_slice_in_dim(targets, start, pts, 1).T, ((0, 0), (0, pad)))
    w_out_p = jnp.pad(w_out, ((0, 0), (0, pad)))
    b_out_p = jnp.pad(b_out, (0, pad))[None]

    pick, pick_t, aim, wgt = lax.optimization_barrier((pick, pick_t, aim, wgt))
    feats_t, hidden, slope, pred = forward(
        pick, own, swapped, same, diag, w_in, b_in[None], w_out_p, b_out_p
    )
    pred = a2a(pred, GROUP)
    dpred, small = crps(pred, aim, wgt)
    dpred = a2a(dpred, GROUP).reshape(MEMBERS * pts, LANES)
    dpre, send = backward(core, dpred, w_out_p, slope, hidden, feats_t, small)
    got = lax.ppermute(send, "c", [(0, 1), (1, 0)])
    d_own, d_swap, d_same, d_diag = latent_grads(dpre, w_in, pick_t)
    got, d_own = lax.optimization_barrier((got, d_own))
    part = pair_sum(core, dpred, dpre, hidden, feats_t, small, got)
    y = lax.axis_index("y")
    up, down = jnp.logical_and(y == 3, h == 0), jnp.logical_and(y == 0, h == 1)
    same_crosses = jnp.logical_or(up, down)
    up, down = jnp.logical_and(y == 3, h == 1), jnp.logical_and(y == 0, h == 0)
    diag_crosses = jnp.logical_or(up, down)
    crossed = lax.ppermute(jnp.where(same_crosses, d_same, d_diag), GRID, CARRY)
    d_same = jnp.where(same_crosses, crossed, d_same)
    d_diag = jnp.where(diag_crosses, crossed, d_diag)
    part = a2a(part, PLANE)
    part, d_swap, d_same, d_diag = lax.optimization_barrier((part, d_swap, d_same, d_diag))
    r_swap = lax.ppermute(d_swap, GRID, back(SWAP))
    r_same = lax.ppermute(d_same, GRID, BACK_SAME)
    r_diag = lax.ppermute(d_diag, GRID, BACK_DIAG)
    def z_stage(x):
        return a2a(total_and_spread(group, x, 8), "z")

    part = lax.cond(counts[0] >= 0, z_stage, lambda x: x[:8], part)
    part, r_swap, r_same, r_diag = lax.optimization_barrier((part, r_swap, r_same, r_diag))
    part = a2a(total_and_spread(group, part, PARTS), PLANE)
    grad_latent = final_latents(side, d_own, r_same, r_swap, r_diag)
    part, grad_latent = lax.optimization_barrier((part, grad_latent))
    got = lax.ppermute(part, "c", [(0, 1), (1, 0)])
    first = unpack(core, part)
    gw_in, gw_out_t, gb_in, gb_out, loss = unpack(1 - core, got, first)
    return (
        grad_latent,
        gw_in,
        gb_in[0],
        gw_out_t.T,
        gb_out[0],
        loss[0, 0],
    )


def solution(mesh):
    fine = Mesh(mesh.devices.reshape(2, 2, 8, 4, 2), ENS + GRID)
    in_specs = (
        P(ENS, GRID, None),
        P(GRID, None),
        P(),
        P(None, GRID),
        P(GRID),
        P(),
        P(),
        P(),
        P(),
        P(),
    )
    out_specs = (P(ENS, GRID, None), P(), P(), P(), P(), P())
    return jax.shard_map(body, mesh=fine, in_specs=in_specs, out_specs=out_specs, check_vma=False)
```

```python
import jax
import jax.numpy as jnp
from jax import lax
from jax.experimental import pallas as pl
from jax.experimental.pallas import tpu as pltpu
from jax.sharding import Mesh, PartitionSpec as P

smooth_sq = 0.0025
smooth_width = 0.05
bf16 = jnp.bfloat16
f32 = jnp.float32

ENS = ("xl", "c")
GRID = ("z", "y", "xh")
GROUP = ("xh", "xl", "c")
PLANE = ("y", "xh", "xl")
MEMBERS = 8
H = 1024
LANES = 128
CHUNK = 256
STEPS = H // CHUNK
ROWS = H + LANES
ROW_GROUPS = 4
PART = ROWS // ROW_GROUPS
PARTS = 16
GB_IN, HIGH, LOW = 100, 101, 102
HIGH_IN_PART = H + HIGH - 3 * PART


def dot(a, b, dims=((1,), (0,))):
    return lax.dot_general(a, b, (dims, ((), ())), preferred_element_type=f32)


def call(kernel, name, flops=0, nbytes=0, trans=0, **kw):
    return pl.pallas_call(
        kernel,
        name=name,
        cost_estimate=pl.CostEstimate(flops=flops, bytes_accessed=nbytes, transcendentals=trans),
        compiler_params=pltpu.CompilerParams(vmem_limit_bytes=24 * 1024 * 1024),
        **kw,
    )


def near(*xs):
    return list(xs)


def pinned(x):
    return pltpu.with_memory_space_constraint(x, pltpu.VMEM)


def far(x):
    return pltpu.with_memory_space_constraint(x, pltpu.HBM)


def out(shape, dtype):
    return jax.ShapeDtypeStruct(shape, dtype)


def ring(shift_odd, shift_even):
    n = 64
    return [(i, (i + (shift_odd if i % 2 else shift_even)) % n) for i in range(n)]


SWAP = ring(-1, 1)
SAME = ring(2, -2)
DIAG = ring(1, -1)


def back(perm):
    return [(b, a) for a, b in perm]


def at(z, y, h):
    return (z % 8 * 4 + y % 4) * 2 + h


PLACES = [(z, y, h) for z in range(8) for y in range(4) for h in range(2)]
BACK_SAME = [(at(z, y, h), at(z, y - 1 if h else y + 1, h)) for z, y, h in PLACES]
BACK_DIAG = [(at(z, y, h), at(z, y + 1 if h else y - 1, 1 - h)) for z, y, h in PLACES]
CARRY = [
    (at(z, y, h), at(z + 1 if y else z - 1, y, h)) for z, y, h in PLACES if y in (0, 3)
]


def a2a(x, axes):
    return lax.all_to_all(x, axes, split_axis=0, concat_axis=0, tiled=True)


def forward_kernel(
    pick, own, swp_a, swp_b, same, diag_a, diag_b, w_in, b_in, w_out, b_out,
    feats_t, hid, slope, pred, w_here, sem
):
    copy = pltpu.make_async_copy(w_in, w_here, sem)
    copy.start()
    n = own.shape[0]
    swp = jnp.concatenate([swp_a[...], swp_b[...]], axis=0)
    diag = jnp.concatenate([diag_a[...], diag_b[...]], axis=0)
    total = dot(pick[:, :n], own[...])
    for k, block in enumerate((swp, same[...], diag)):
        total = total + dot(pick[:, (k + 1) * n : (k + 2) * n], block)
    feats = (total / 3.0).astype(bf16)
    feats_t[...] = feats.T
    copy.wait()
    v = dot(feats, w_here[...]) + b_in[...]
    cdf = 0.5 * (1.0 + lax.erf(v * 0.7071067811865476))
    slope[...] = (cdf + v * jnp.exp(-0.5 * v * v) * 0.3989422804014327).astype(bf16)
    h = (v * cdf).astype(bf16)
    hid[...] = h
    p = dot(h, w_out[...]) + b_out[...]
    pts = pred.shape[1]
    for i in range(MEMBERS):
        pred[i] = p[i * pts : (i + 1) * pts]


def forward(pick, nodes, w_in, b_in, w_out, b_out):
    m = pick.shape[0]
    return call(
        forward_kernel,
        "forward",
        flops=2 * m * H * (2 * H + LANES),
        nbytes=12 * 2**20,
        trans=2 * m * H,
        in_specs=[pl.BlockSpec(memory_space=pltpu.VMEM)] * 7
        + [pl.BlockSpec(memory_space=pl.ANY)]
        + [pl.BlockSpec(memory_space=pltpu.VMEM)] * 3,
        scratch_shapes=[pltpu.VMEM((H, H), bf16), pltpu.SemaphoreType.DMA],
        out_shape=[
            out((H, m), bf16),
            out((m, H), bf16),
            out((m, H), bf16),
            jax.ShapeDtypeStruct((MEMBERS, m // MEMBERS, LANES), f32),
        ],
    )(pick, *nodes, far(w_in), b_in, w_out, b_out)


def crps_kernel(pred, aim, wgt, dpred, small):
    mm = float(MEMBERS)
    pts = pred.shape[1]
    gb = jnp.zeros((1, LANES), f32)
    loss = jnp.zeros((1, LANES), f32)
    for r in range(0, pts, 16):
        p = [pred[i, r : r + 16, :] for i in range(MEMBERS)]
        pair = [jnp.zeros((16, LANES), f32) for _ in range(MEMBERS)]
        gaps = jnp.zeros((16, LANES), f32)
        hits = jnp.zeros((16, LANES), f32)
        for i in range(MEMBERS):
            for j in range(i + 1, MEMBERS):
                d = p[i] - p[j]
                sq = d * d + smooth_sq
                inv = lax.rsqrt(sq)
                gaps = gaps + (sq * inv - smooth_width)
                pair[i] = pair[i] + d * inv
                pair[j] = pair[j] - d * inv
        w = wgt[r : r + 16, :]
        t = aim[r : r + 16, :]
        g_sum = jnp.zeros((16, LANES), f32)
        for i in range(MEMBERS):
            d = p[i] - t
            sq = d * d + smooth_sq
            inv = lax.rsqrt(sq)
            hits = hits + (sq * inv - smooth_width)
            g = w * (d * inv / mm - pair[i] / (mm * (mm - 1.0)))
            g_sum = g_sum + g
            dpred[i, r : r + 16, :] = g.astype(bf16)
        gb = gb + jnp.sum(g_sum, axis=0, keepdims=True)
        loss = loss + jnp.sum(w * (hits / mm - gaps / (mm * (mm - 1.0))), axis=0, keepdims=True)
    small[:, :LANES] = gb
    small[:, LANES:] = loss


def crps(pred, aim, wgt):
    pts = aim.shape[0]
    return call(
        crps_kernel,
        "crps",
        flops=40 * 36 * pts * LANES,
        nbytes=2**19,
        trans=36 * pts * LANES,
        out_shape=[
            jax.ShapeDtypeStruct((MEMBERS, pts, LANES), bf16),
            out((1, 2 * LANES), f32),
        ],
    )(*near(pred, aim, wgt))


def packed(half, feats_t, dpre, dpred, hid, small):
    cols = pl.ds(pl.multiple_of(half * (H // 2), H // 2), H // 2)
    d = dpre[:, cols]
    gb_in = jnp.sum(d.astype(f32), axis=0, keepdims=True)
    foot = dot(dpred[...], hid[:, cols], ((0,), (0,)))
    row = lax.broadcasted_iota(jnp.int32, foot.shape, 0)
    s = jnp.concatenate([small[...], jnp.zeros_like(small[...])], axis=1)
    s = jnp.where(half == 0, s, 0.0)
    high = s.astype(bf16).astype(f32)
    foot = jnp.where(row == GB_IN, gb_in, foot)
    foot = jnp.where(row == HIGH, high, foot)
    foot = jnp.where(row == LOW, s - high, foot)
    main = dot(feats_t[...], d)
    for g in range(ROW_GROUPS):
        lanes = slice(g * LANES, (g + 1) * LANES)
        for r in range(ROW_GROUPS):
            block = main[r * PART : (r + 1) * PART, lanes]
            if r == ROW_GROUPS - 1:
                block = jnp.concatenate([block, foot[:, lanes]], axis=0)
            yield g * ROW_GROUPS + r, block


def backward_kernel(core, dpred, w_out, slope, hid, feats_t, small, dpre, send):
    d = dot(dpred[...], w_out[...], ((1,), (1,))) * slope[...].astype(f32)
    dpre[...] = d.astype(bf16)
    for i, block in packed(1 - core[0], feats_t, dpre, dpred, hid, small):
        send[i] = block.astype(bf16)


def backward(core, dpred, w_out, slope, hid, feats_t, small):
    m = dpred.shape[0]
    return call(
        backward_kernel,
        "backward",
        flops=m * H * (H + 4 * LANES),
        nbytes=6 * 2**20,
        in_specs=[pl.BlockSpec(memory_space=pltpu.SMEM)]
        + [pl.BlockSpec(memory_space=pltpu.VMEM)] * 6,
        out_shape=[out((m, H), bf16), out((PARTS, PART, LANES), bf16)],
    )(core, *near(dpred, w_out, slope, hid, feats_t, small))


def latent_kernel(dpre, w_in, pick_t, own, swp, same, diag):
    d = (dot(dpre[...], w_in[...], ((1,), (1,))) / 3.0).astype(bf16)
    n = own.shape[0]
    for k, ref in enumerate((own, swp, same, diag)):
        ref[...] = dot(pick_t[k * n : (k + 1) * n, :], d).astype(ref.dtype)


def latent_grads(dpre, w_in, pick_t):
    m = dpre.shape[0]
    n = pick_t.shape[0] // 4
    return call(
        latent_kernel,
        "latent_grads",
        flops=4 * m * H * H,
        nbytes=8 * 2**20,
        out_shape=[pltpu.HBM((n, H), f32)] + [pltpu.HBM((n, H), bf16)] * 3,
    )(*near(dpre, w_in, pick_t))


def resplit(total):
    row = lax.broadcasted_iota(jnp.int32, total.shape, 0)
    both = total[HIGH_IN_PART : HIGH_IN_PART + 1] + total[HIGH_IN_PART + 1 : HIGH_IN_PART + 2]
    high = both.astype(bf16).astype(f32)
    total_high = jnp.where(row == HIGH_IN_PART, high, total)
    return jnp.where(row == HIGH_IN_PART + 1, both - high, total_high).astype(bf16)


def pair_kernel(core, dpred, dpre, hid, feats_t, small, got, part):
    for i, block in packed(core[0], feats_t, dpre, dpred, hid, small):
        total = block + got[i].astype(f32)
        if i % ROW_GROUPS == ROW_GROUPS - 1:
            total = resplit(total)
        part[i] = total.astype(bf16)


def pair_sum(core, dpred, dpre, hid, feats_t, small, got):
    m = dpred.shape[0]
    return call(
        pair_kernel,
        "pair_sum",
        flops=m * H * (H + 2 * LANES),
        nbytes=6 * 2**20,
        in_specs=[pl.BlockSpec(memory_space=pltpu.SMEM)]
        + [pl.BlockSpec(memory_space=pltpu.VMEM)] * 6,
        out_shape=jax.ShapeDtypeStruct(got.shape, bf16),
    )(core, *near(dpred, dpre, hid, feats_t, small, got))


def total_kernel(group, parts, copies):
    total = parts[0].astype(f32)
    for i in range(1, parts.shape[0]):
        total = total + parts[i].astype(f32)
    last = group[0] == ROW_GROUPS - 1
    done = jnp.where(last, resplit(total).astype(f32), total).astype(bf16)
    for i in range(copies.shape[0]):
        copies[i] = done


def total_and_spread(group, parts, copies):
    n = parts.shape[0]
    return call(
        total_kernel,
        "total",
        flops=n * PART * LANES,
        nbytes=2 * (n + copies) * PART * LANES,
        in_specs=[
            pl.BlockSpec(memory_space=pltpu.SMEM),
            pl.BlockSpec(memory_space=pltpu.VMEM),
        ],
        out_shape=jax.ShapeDtypeStruct((copies, PART, LANES), bf16),
    )(group, pinned(parts))


def unpack_half(half, parts, gw_in, gw_out_t, gb_in, keep):
    j = pl.program_id(0)
    for g in range(2):
        lanes = slice(g * LANES, (g + 1) * LANES)
        base = g * ROW_GROUPS
        for r in range(ROW_GROUPS - 1):
            gw_in[r * PART : (r + 1) * PART, lanes] = parts[base + r].astype(f32)
        r = ROW_GROUPS - 1
        gw_in[r * PART :, lanes] = parts[base + r, : H - r * PART, :].astype(f32)
        foot = parts[base + r, H - r * PART :, :].astype(f32)
        gw_out_t[:, lanes] = foot[:GB_IN]
        gb_in[:, lanes] = foot[GB_IN : GB_IN + 1]
        small = foot[HIGH : HIGH + 1] + foot[LOW : LOW + 1]

        @pl.when(jnp.logical_and(j == 0, half[0] == 0))
        def _():
            keep(g, small)


def first_kernel(half, parts, gw_in, gw_out_t, gb_in, gb_out, loss):
    @pl.when(pl.program_id(0) == 0)
    def _():
        gb_out[...] = jnp.zeros_like(gb_out)
        loss[...] = jnp.zeros_like(loss)

    def keep(g, small):
        if g == 0:
            gb_out[...] = small[:, :GB_IN]
        else:
            loss[...] = jnp.sum(small, axis=1, keepdims=True)

    unpack_half(half, parts, gw_in, gw_out_t, gb_in, keep)


def second_kernel(half, parts, a, b, c, gb_one, loss_one, gw_in, gw_out_t, gb_in, gb_out, loss):
    del a, b, c

    @pl.when(pl.program_id(0) == 0)
    def _():
        gb_out[...] = gb_one[...]
        loss[...] = loss_one[...]

    def keep(g, small):
        if g == 0:
            gb_out[...] = small[:, :GB_IN]
        else:
            loss[...] = jnp.sum(small, axis=1, keepdims=True)

    unpack_half(half, parts, gw_in, gw_out_t, gb_in, keep)


def unpack(half, parts, first=None):
    cols = lambda j, half: (0, 2 * half[0] + j)
    whole = lambda j, half: (0, 0)
    anywhere = pl.BlockSpec(memory_space=pl.ANY)
    smalls = [pl.BlockSpec((1, GB_IN), whole), pl.BlockSpec((1, 1), whole)]
    more = [] if first is None else [anywhere] * 3 + smalls
    return call(
        first_kernel if first is None else second_kernel,
        "unpack_first" if first is None else "unpack_second",
        nbytes=4 * 2**20,
        grid_spec=pltpu.PrefetchScalarGridSpec(
            num_scalar_prefetch=1,
            grid=(2,),
            in_specs=[
                pl.BlockSpec((2 * ROW_GROUPS, PART, LANES), lambda j, half: (j, 0, 0)),
            ]
            + more,
            out_specs=[
                pl.BlockSpec((H, CHUNK), cols),
                pl.BlockSpec((GB_IN, CHUNK), cols),
                pl.BlockSpec((1, CHUNK), cols),
            ]
            + smalls,
        ),
        out_shape=[
            jax.ShapeDtypeStruct((H, H), f32),
            jax.ShapeDtypeStruct((GB_IN, H), f32),
            jax.ShapeDtypeStruct((1, H), f32),
            jax.ShapeDtypeStruct((1, GB_IN), f32),
            jax.ShapeDtypeStruct((1, 1), f32),
        ],
        input_output_aliases={} if first is None else {2: 0, 3: 1, 4: 2},
    )(half, parts, *([] if first is None else first))


def final_kernel(side, own, same, swp, diag, both):
    j = pl.program_id(0)

    @pl.when(j == 0)
    def _():
        both[0] = (own[...] + same[...].astype(f32)).astype(bf16)

    @pl.when(j == 1)
    def _():
        both[0] = (swp[...].astype(f32) + diag[...].astype(f32)).astype(bf16)


def final_latents(side, own, same, swp, diag):
    n = own.shape[0]
    whole = lambda j, side: (0, 0)
    block = pl.BlockSpec((n, H), whole)
    return call(
        final_kernel,
        "final_latents",
        nbytes=5 * 2**20,
        grid_spec=pltpu.PrefetchScalarGridSpec(
            num_scalar_prefetch=1,
            grid=(2,),
            in_specs=[block] * 4,
            out_specs=pl.BlockSpec(
                (1, n, H), lambda j, side: (jnp.where(j == 0, side[0], 1 - side[0]), 0, 0)
            ),
        ),
        out_shape=jax.ShapeDtypeStruct((2, n, H), bf16),
    )(side, own, same, swp, diag)


def body(latent, edge_src, counts, targets, area, var_weight, w_in, b_in, w_out, b_out):
    l_tile, width = latent.shape[1:]
    g_tile, k_edges = edge_src.shape
    n_vars = w_out.shape[1]
    h = lax.axis_index("xh")
    core = lax.axis_index("c")
    pair = lax.axis_index(("z", "y"))
    tile = 2 * pair + h
    quarter = lax.axis_index(ENS)
    pts = g_tile // 4
    side = jnp.reshape(h, (1,)).astype(jnp.int32)
    core = jnp.reshape(core, (1,)).astype(jnp.int32)
    group = lax.rem(lax.axis_index(PLANE), ROW_GROUPS)
    group = jnp.reshape(group, (1,)).astype(jnp.int32)

    half = l_tile // 2
    oth_a = lax.dynamic_slice(latent, (1 - h, 0, 0), (1, half, width))[0]
    edges_there = lax.ppermute(edge_src, GRID, SWAP)
    swap_a = lax.ppermute(oth_a, GRID, SWAP)
    later, edges_there, edge_src, targets, area, counts, w_out, b_out = lax.optimization_barrier(
        (latent, edges_there, edge_src, targets, area, counts, w_out, b_out)
    )
    own = lax.dynamic_index_in_dim(later, h, 0, keepdims=False)
    oth_b = lax.dynamic_slice(later, (1 - h, half, 0), (1, half, width))[0]
    swap_b = lax.ppermute(oth_b, GRID, SWAP)
    diag_b = lax.ppermute(oth_b, GRID, DIAG)
    same = lax.ppermute(own, GRID, SAME)
    diag_a = lax.ppermute(swap_a, GRID, back(SAME))

    edges = jnp.where(
        h == 0,
        jnp.concatenate([edge_src, edges_there], axis=0),
        jnp.concatenate([edges_there, edge_src], axis=0),
    )
    step = edges // l_tile - 2 * pair
    block = jnp.mod(jnp.where(h == 0, step, 1 - step), 4)
    local = block * l_tile + jnp.mod(edges, l_tile)
    nodes = lax.broadcasted_iota(jnp.int32, (2 * g_tile, 4 * l_tile), 1)
    nodes_t = lax.broadcasted_iota(jnp.int32, (4 * l_tile, 2 * g_tile), 0)
    pick = jnp.zeros((2 * g_tile, 4 * l_tile), f32)
    pick_t = jnp.zeros((4 * l_tile, 2 * g_tile), f32)
    for k in range(k_edges):
        pick = pick + (local[:, k : k + 1] == nodes).astype(f32)
        pick_t = pick_t + (local[:, k][None, :] == nodes_t).astype(f32)
    pick = pick.astype(bf16)
    pick_t = pick_t.astype(bf16)

    start = quarter * pts
    point = start + jnp.arange(pts, dtype=jnp.int32)
    valid = (point < counts[tile]).astype(f32)
    pad = LANES - n_vars
    var_weight = jnp.pad(var_weight, (0, pad))
    wgt = (lax.dynamic_slice_in_dim(area, start, pts, 0) * valid)[:, None] * var_weight[None, :]
    aim = jnp.pad(lax.dynamic_slice_in_dim(targets, start, pts, 1).T, ((0, 0), (0, pad)))
    w_out_p = jnp.pad(w_out, ((0, 0), (0, pad)))
    b_out_p = jnp.pad(b_out, (0, pad))[None]

    pick, pick_t, aim, wgt = lax.optimization_barrier((pick, pick_t, aim, wgt))
    feats_t, hidden, slope, pred = forward(
        pick, (own, swap_a, swap_b, same, diag_a, diag_b), w_in, b_in[None], w_out_p, b_out_p
    )
    pred = a2a(pred, GROUP)
    dpred, small = crps(pred, aim, wgt)
    dpred = a2a(dpred, GROUP).reshape(MEMBERS * pts, LANES)
    dpre, send = backward(core, dpred, w_out_p, slope, hidden, feats_t, small)
    got = lax.ppermute(send, "c", [(0, 1), (1, 0)])
    d_own, d_swap, d_same, d_diag = latent_grads(dpre, w_in, pick_t)
    got, d_own = lax.optimization_barrier((got, d_own))
    part = pair_sum(core, dpred, dpre, hidden, feats_t, small, got)
    y = lax.axis_index("y")
    up, down = jnp.logical_and(y == 3, h == 0), jnp.logical_and(y == 0, h == 1)
    same_crosses = jnp.logical_or(up, down)
    up, down = jnp.logical_and(y == 3, h == 1), jnp.logical_and(y == 0, h == 0)
    diag_crosses = jnp.logical_or(up, down)
    crossed = lax.ppermute(jnp.where(same_crosses, d_same, d_diag), GRID, CARRY)
    d_same = jnp.where(same_crosses, crossed, d_same)
    d_diag = jnp.where(diag_crosses, crossed, d_diag)
    part = a2a(part, PLANE)
    part, d_swap, d_same, d_diag = lax.optimization_barrier((part, d_swap, d_same, d_diag))
    r_swap = lax.ppermute(d_swap, GRID, back(SWAP))
    r_same = lax.ppermute(d_same, GRID, BACK_SAME)
    r_diag = lax.ppermute(d_diag, GRID, BACK_DIAG)
    def z_stage(x):
        return a2a(total_and_spread(group, x, 8), "z")

    part = lax.cond(counts[0] >= 0, z_stage, lambda x: x[:8], part)
    part, r_swap, r_same, r_diag = lax.optimization_barrier((part, r_swap, r_same, r_diag))
    part = a2a(total_and_spread(group, part, PARTS), PLANE)
    grad_latent = final_latents(side, d_own, r_same, r_swap, r_diag)
    part, grad_latent = lax.optimization_barrier((part, grad_latent))
    got = lax.ppermute(part, "c", [(0, 1), (1, 0)])
    first = unpack(core, part)
    gw_in, gw_out_t, gb_in, gb_out, loss = unpack(1 - core, got, first)
    return (
        grad_latent,
        gw_in,
        gb_in[0],
        gw_out_t.T,
        gb_out[0],
        loss[0, 0],
    )


def solution(mesh):
    fine = Mesh(mesh.devices.reshape(2, 2, 8, 4, 2), ENS + GRID)
    in_specs = (
        P(ENS, GRID, None),
        P(GRID, None),
        P(),
        P(None, GRID),
        P(GRID),
        P(),
        P(),
        P(),
        P(),
        P(),
    )
    out_specs = (P(ENS, GRID, None), P(), P(), P(), P(), P())
    return jax.shard_map(body, mesh=fine, in_specs=in_specs, out_specs=out_specs, check_vma=False)
```

```python
import jax
import jax.numpy as jnp
from jax import lax
from jax.experimental import pallas as pl
from jax.experimental.pallas import tpu as pltpu
from jax.sharding import Mesh, PartitionSpec as P

smooth_sq = 0.0025
smooth_width = 0.05
bf16 = jnp.bfloat16
f32 = jnp.float32

ENS = ("xl", "c")
GRID = ("z", "y", "xh")
GROUP = ("xh", "xl", "c")
PLANE = ("y", "xh", "xl")
MEMBERS = 8
H = 1024
LANES = 128
CHUNK = 256
STEPS = H // CHUNK
ROWS = H + LANES
ROW_GROUPS = 4
PART = ROWS // ROW_GROUPS
PARTS = 16
GB_IN, HIGH, LOW = 100, 101, 102
HIGH_IN_PART = H + HIGH - 3 * PART


def dot(a, b, dims=((1,), (0,))):
    return lax.dot_general(a, b, (dims, ((), ())), preferred_element_type=f32)


def call(kernel, name, flops=0, nbytes=0, trans=0, **kw):
    return pl.pallas_call(
        kernel,
        name=name,
        cost_estimate=pl.CostEstimate(flops=flops, bytes_accessed=nbytes, transcendentals=trans),
        compiler_params=pltpu.CompilerParams(vmem_limit_bytes=24 * 1024 * 1024),
        **kw,
    )


def near(*xs):
    return list(xs)


def pinned(x):
    return pltpu.with_memory_space_constraint(x, pltpu.VMEM)


def far(x):
    return pltpu.with_memory_space_constraint(x, pltpu.HBM)


def out(shape, dtype):
    return jax.ShapeDtypeStruct(shape, dtype)


def ring(shift_odd, shift_even):
    n = 64
    return [(i, (i + (shift_odd if i % 2 else shift_even)) % n) for i in range(n)]


SWAP = ring(-1, 1)
SAME = ring(2, -2)
DIAG = ring(1, -1)


def back(perm):
    return [(b, a) for a, b in perm]


def at(z, y, h):
    return (z % 8 * 4 + y % 4) * 2 + h


PLACES = [(z, y, h) for z in range(8) for y in range(4) for h in range(2)]
BACK_SAME = [(at(z, y, h), at(z, y - 1 if h else y + 1, h)) for z, y, h in PLACES]
BACK_DIAG = [(at(z, y, h), at(z, y + 1 if h else y - 1, 1 - h)) for z, y, h in PLACES]
CARRY = [
    (at(z, y, h), at(z + 1 if y else z - 1, y, h)) for z, y, h in PLACES if y in (0, 3)
]


def a2a(x, axes):
    return lax.all_to_all(x, axes, split_axis=0, concat_axis=0, tiled=True)


def forward_kernel(pick, own, swp, same, diag, w_in, b_in, w_out, b_out, feats_t, hid, slope, pred, w_here, sem):
    n = own.shape[0]
    copy = pltpu.make_async_copy(w_in, w_here, sem)
    copy.start()
    total = dot(pick[:, :n], own[...])
    for k, ref in enumerate((swp, same, diag)):
        total = total + dot(pick[:, (k + 1) * n : (k + 2) * n], ref[...])
    feats = (total / 3.0).astype(bf16)
    feats_t[...] = feats.T
    copy.wait()
    v = dot(feats, w_here[...]) + b_in[...]
    cdf = 0.5 * (1.0 + lax.erf(v * 0.7071067811865476))
    slope[...] = (cdf + v * jnp.exp(-0.5 * v * v) * 0.3989422804014327).astype(bf16)
    h = (v * cdf).astype(bf16)
    hid[...] = h
    p = dot(h, w_out[...]) + b_out[...]
    pts = pred.shape[1]
    for i in range(MEMBERS):
        pred[i] = p[i * pts : (i + 1) * pts]


def forward(pick, own, swp, same, diag, w_in, b_in, w_out, b_out):
    m = pick.shape[0]
    return call(
        forward_kernel,
        "forward",
        flops=2 * m * H * (2 * H + LANES),
        nbytes=12 * 2**20,
        trans=2 * m * H,
        in_specs=[pl.BlockSpec(memory_space=pltpu.VMEM)] * 5
        + [pl.BlockSpec(memory_space=pl.ANY)]
        + [pl.BlockSpec(memory_space=pltpu.VMEM)] * 3,
        scratch_shapes=[pltpu.VMEM((H, H), bf16), pltpu.SemaphoreType.DMA],
        out_shape=[
            out((H, m), bf16),
            out((m, H), bf16),
            out((m, H), bf16),
            jax.ShapeDtypeStruct((MEMBERS, m // MEMBERS, LANES), f32),
        ],
    )(*near(pick, own, swp, same, diag), far(w_in), *near(b_in, w_out, b_out))


def crps_kernel(pred, aim, wgt, dpred, small):
    mm = float(MEMBERS)
    pts = pred.shape[1]
    gb = jnp.zeros((1, LANES), f32)
    loss = jnp.zeros((1, LANES), f32)
    for r in range(0, pts, 16):
        p = [pred[i, r : r + 16, :] for i in range(MEMBERS)]
        pair = [jnp.zeros((16, LANES), f32) for _ in range(MEMBERS)]
        gaps = jnp.zeros((16, LANES), f32)
        hits = jnp.zeros((16, LANES), f32)
        for i in range(MEMBERS):
            for j in range(i + 1, MEMBERS):
                d = p[i] - p[j]
                sq = d * d + smooth_sq
                inv = lax.rsqrt(sq)
                gaps = gaps + (sq * inv - smooth_width)
                pair[i] = pair[i] + d * inv
                pair[j] = pair[j] - d * inv
        w = wgt[r : r + 16, :]
        t = aim[r : r + 16, :]
        g_sum = jnp.zeros((16, LANES), f32)
        for i in range(MEMBERS):
            d = p[i] - t
            sq = d * d + smooth_sq
            inv = lax.rsqrt(sq)
            hits = hits + (sq * inv - smooth_width)
            g = w * (d * inv / mm - pair[i] / (mm * (mm - 1.0)))
            g_sum = g_sum + g
            dpred[i, r : r + 16, :] = g.astype(bf16)
        gb = gb + jnp.sum(g_sum, axis=0, keepdims=True)
        loss = loss + jnp.sum(w * (hits / mm - gaps / (mm * (mm - 1.0))), axis=0, keepdims=True)
    small[:, :LANES] = gb
    small[:, LANES:] = loss


def crps(pred, aim, wgt):
    pts = aim.shape[0]
    return call(
        crps_kernel,
        "crps",
        flops=40 * 36 * pts * LANES,
        nbytes=2**19,
        trans=36 * pts * LANES,
        out_shape=[
            jax.ShapeDtypeStruct((MEMBERS, pts, LANES), bf16),
            out((1, 2 * LANES), f32),
        ],
    )(*near(pred, aim, wgt))


def packed(half, feats_t, dpre, dpred, hid, small):
    cols = pl.ds(pl.multiple_of(half * (H // 2), H // 2), H // 2)
    d = dpre[:, cols]
    gb_in = jnp.sum(d.astype(f32), axis=0, keepdims=True)
    foot = dot(dpred[...], hid[:, cols], ((0,), (0,)))
    row = lax.broadcasted_iota(jnp.int32, foot.shape, 0)
    s = jnp.concatenate([small[...], jnp.zeros_like(small[...])], axis=1)
    s = jnp.where(half == 0, s, 0.0)
    high = s.astype(bf16).astype(f32)
    foot = jnp.where(row == GB_IN, gb_in, foot)
    foot = jnp.where(row == HIGH, high, foot)
    foot = jnp.where(row == LOW, s - high, foot)
    main = dot(feats_t[...], d)
    for g in range(ROW_GROUPS):
        lanes = slice(g * LANES, (g + 1) * LANES)
        for r in range(ROW_GROUPS):
            block = main[r * PART : (r + 1) * PART, lanes]
            if r == ROW_GROUPS - 1:
                block = jnp.concatenate([block, foot[:, lanes]], axis=0)
            yield g * ROW_GROUPS + r, block


def backward_kernel(core, dpred, w_out, slope, hid, feats_t, small, dpre, send):
    d = dot(dpred[...], w_out[...], ((1,), (1,))) * slope[...].astype(f32)
    dpre[...] = d.astype(bf16)
    for i, block in packed(1 - core[0], feats_t, dpre, dpred, hid, small):
        send[i] = block.astype(bf16)


def backward(core, dpred, w_out, slope, hid, feats_t, small):
    m = dpred.shape[0]
    return call(
        backward_kernel,
        "backward",
        flops=m * H * (H + 4 * LANES),
        nbytes=6 * 2**20,
        in_specs=[pl.BlockSpec(memory_space=pltpu.SMEM)]
        + [pl.BlockSpec(memory_space=pltpu.VMEM)] * 6,
        out_shape=[out((m, H), bf16), out((PARTS, PART, LANES), bf16)],
    )(core, *near(dpred, w_out, slope, hid, feats_t, small))


def latent_kernel(dpre, w_in, pick_t, own, swp, same, diag):
    d = (dot(dpre[...], w_in[...], ((1,), (1,))) / 3.0).astype(bf16)
    n = own.shape[0]
    for k, ref in enumerate((own, swp, same, diag)):
        ref[...] = dot(pick_t[k * n : (k + 1) * n, :], d).astype(ref.dtype)


def latent_grads(dpre, w_in, pick_t):
    m = dpre.shape[0]
    n = pick_t.shape[0] // 4
    return call(
        latent_kernel,
        "latent_grads",
        flops=4 * m * H * H,
        nbytes=8 * 2**20,
        out_shape=[pltpu.HBM((n, H), f32)] + [pltpu.HBM((n, H), bf16)] * 3,
    )(*near(dpre, w_in, pick_t))


def resplit(total):
    row = lax.broadcasted_iota(jnp.int32, total.shape, 0)
    both = total[HIGH_IN_PART : HIGH_IN_PART + 1] + total[HIGH_IN_PART + 1 : HIGH_IN_PART + 2]
    high = both.astype(bf16).astype(f32)
    total_high = jnp.where(row == HIGH_IN_PART, high, total)
    return jnp.where(row == HIGH_IN_PART + 1, both - high, total_high).astype(bf16)


def pair_kernel(core, dpred, dpre, hid, feats_t, small, got, part):
    for i, block in packed(core[0], feats_t, dpre, dpred, hid, small):
        total = block + got[i].astype(f32)
        if i % ROW_GROUPS == ROW_GROUPS - 1:
            total = resplit(total)
        part[i] = total.astype(bf16)


def pair_sum(core, dpred, dpre, hid, feats_t, small, got):
    m = dpred.shape[0]
    return call(
        pair_kernel,
        "pair_sum",
        flops=m * H * (H + 2 * LANES),
        nbytes=6 * 2**20,
        in_specs=[pl.BlockSpec(memory_space=pltpu.SMEM)]
        + [pl.BlockSpec(memory_space=pltpu.VMEM)] * 6,
        out_shape=jax.ShapeDtypeStruct(got.shape, bf16),
    )(core, *near(dpred, dpre, hid, feats_t, small, got))


def total_kernel(group, parts, copies):
    total = parts[0].astype(f32)
    for i in range(1, parts.shape[0]):
        total = total + parts[i].astype(f32)
    last = group[0] == ROW_GROUPS - 1
    done = jnp.where(last, resplit(total).astype(f32), total).astype(bf16)
    for i in range(copies.shape[0]):
        copies[i] = done


def total_and_spread(group, parts, copies):
    n = parts.shape[0]
    return call(
        total_kernel,
        "total",
        flops=n * PART * LANES,
        nbytes=2 * (n + copies) * PART * LANES,
        in_specs=[
            pl.BlockSpec(memory_space=pltpu.SMEM),
            pl.BlockSpec(memory_space=pltpu.VMEM),
        ],
        out_shape=jax.ShapeDtypeStruct((copies, PART, LANES), bf16),
    )(group, pinned(parts))


def unpack_half(half, parts, gw_in, gw_out_t, gb_in, keep):
    j = pl.program_id(0)
    for g in range(2):
        lanes = slice(g * LANES, (g + 1) * LANES)
        base = g * ROW_GROUPS
        for r in range(ROW_GROUPS - 1):
            gw_in[r * PART : (r + 1) * PART, lanes] = parts[base + r].astype(f32)
        r = ROW_GROUPS - 1
        gw_in[r * PART :, lanes] = parts[base + r, : H - r * PART, :].astype(f32)
        foot = parts[base + r, H - r * PART :, :].astype(f32)
        gw_out_t[:, lanes] = foot[:GB_IN]
        gb_in[:, lanes] = foot[GB_IN : GB_IN + 1]
        small = foot[HIGH : HIGH + 1] + foot[LOW : LOW + 1]

        @pl.when(jnp.logical_and(j == 0, half[0] == 0))
        def _():
            keep(g, small)


def first_kernel(half, parts, gw_in, gw_out_t, gb_in, gb_out, loss):
    @pl.when(pl.program_id(0) == 0)
    def _():
        gb_out[...] = jnp.zeros_like(gb_out)
        loss[...] = jnp.zeros_like(loss)

    def keep(g, small):
        if g == 0:
            gb_out[...] = small[:, :GB_IN]
        else:
            loss[...] = jnp.sum(small, axis=1, keepdims=True)

    unpack_half(half, parts, gw_in, gw_out_t, gb_in, keep)


def second_kernel(half, parts, a, b, c, gb_one, loss_one, gw_in, gw_out_t, gb_in, gb_out, loss):
    del a, b, c

    @pl.when(pl.program_id(0) == 0)
    def _():
        gb_out[...] = gb_one[...]
        loss[...] = loss_one[...]

    def keep(g, small):
        if g == 0:
            gb_out[...] = small[:, :GB_IN]
        else:
            loss[...] = jnp.sum(small, axis=1, keepdims=True)

    unpack_half(half, parts, gw_in, gw_out_t, gb_in, keep)


def unpack(half, parts, first=None):
    cols = lambda j, half: (0, 2 * half[0] + j)
    whole = lambda j, half: (0, 0)
    anywhere = pl.BlockSpec(memory_space=pl.ANY)
    smalls = [pl.BlockSpec((1, GB_IN), whole), pl.BlockSpec((1, 1), whole)]
    more = [] if first is None else [anywhere] * 3 + smalls
    return call(
        first_kernel if first is None else second_kernel,
        "unpack_first" if first is None else "unpack_second",
        nbytes=4 * 2**20,
        grid_spec=pltpu.PrefetchScalarGridSpec(
            num_scalar_prefetch=1,
            grid=(2,),
            in_specs=[
                pl.BlockSpec((2 * ROW_GROUPS, PART, LANES), lambda j, half: (j, 0, 0)),
            ]
            + more,
            out_specs=[
                pl.BlockSpec((H, CHUNK), cols),
                pl.BlockSpec((GB_IN, CHUNK), cols),
                pl.BlockSpec((1, CHUNK), cols),
            ]
            + smalls,
        ),
        out_shape=[
            jax.ShapeDtypeStruct((H, H), f32),
            jax.ShapeDtypeStruct((GB_IN, H), f32),
            jax.ShapeDtypeStruct((1, H), f32),
            jax.ShapeDtypeStruct((1, GB_IN), f32),
            jax.ShapeDtypeStruct((1, 1), f32),
        ],
        input_output_aliases={} if first is None else {2: 0, 3: 1, 4: 2},
    )(half, parts, *([] if first is None else first))


def final_kernel(side, own, same, swp, diag, both):
    j = pl.program_id(0)

    @pl.when(j == 0)
    def _():
        both[0] = (own[...] + same[...].astype(f32)).astype(bf16)

    @pl.when(j == 1)
    def _():
        both[0] = (swp[...].astype(f32) + diag[...].astype(f32)).astype(bf16)


def final_latents(side, own, same, swp, diag):
    n = own.shape[0]
    whole = lambda j, side: (0, 0)
    block = pl.BlockSpec((n, H), whole)
    return call(
        final_kernel,
        "final_latents",
        nbytes=5 * 2**20,
        grid_spec=pltpu.PrefetchScalarGridSpec(
            num_scalar_prefetch=1,
            grid=(2,),
            in_specs=[block] * 4,
            out_specs=pl.BlockSpec(
                (1, n, H), lambda j, side: (jnp.where(j == 0, side[0], 1 - side[0]), 0, 0)
            ),
        ),
        out_shape=jax.ShapeDtypeStruct((2, n, H), bf16),
    )(side, own, same, swp, diag)


def body(latent, edge_src, counts, targets, area, var_weight, w_in, b_in, w_out, b_out):
    l_tile = latent.shape[1]
    g_tile, k_edges = edge_src.shape
    n_vars = w_out.shape[1]
    h = lax.axis_index("xh")
    core = lax.axis_index("c")
    pair = lax.axis_index(("z", "y"))
    tile = 2 * pair + h
    quarter = lax.axis_index(ENS)
    pts = g_tile // 4
    side = jnp.reshape(h, (1,)).astype(jnp.int32)
    core = jnp.reshape(core, (1,)).astype(jnp.int32)
    group = lax.rem(lax.axis_index(PLANE), ROW_GROUPS)
    group = jnp.reshape(group, (1,)).astype(jnp.int32)

    own = lax.dynamic_index_in_dim(latent, h, 0, keepdims=False)
    oth = lax.dynamic_index_in_dim(latent, 1 - h, 0, keepdims=False)
    edges_there = lax.ppermute(edge_src, GRID, SWAP)
    swapped = lax.ppermute(oth, GRID, SWAP)
    diag = lax.ppermute(oth, GRID, DIAG)
    same = lax.ppermute(own, GRID, SAME)

    edges = jnp.where(
        h == 0,
        jnp.concatenate([edge_src, edges_there], axis=0),
        jnp.concatenate([edges_there, edge_src], axis=0),
    )
    step = edges // l_tile - 2 * pair
    block = jnp.mod(jnp.where(h == 0, step, 1 - step), 4)
    local = block * l_tile + jnp.mod(edges, l_tile)
    nodes = lax.broadcasted_iota(jnp.int32, (2 * g_tile, 4 * l_tile), 1)
    nodes_t = lax.broadcasted_iota(jnp.int32, (4 * l_tile, 2 * g_tile), 0)
    pick = jnp.zeros((2 * g_tile, 4 * l_tile), f32)
    pick_t = jnp.zeros((4 * l_tile, 2 * g_tile), f32)
    for k in range(k_edges):
        pick = pick + (local[:, k : k + 1] == nodes).astype(f32)
        pick_t = pick_t + (local[:, k][None, :] == nodes_t).astype(f32)
    pick = pick.astype(bf16)
    pick_t = pick_t.astype(bf16)

    start = quarter * pts
    point = start + jnp.arange(pts, dtype=jnp.int32)
    valid = (point < counts[tile]).astype(f32)
    pad = LANES - n_vars
    var_weight = jnp.pad(var_weight, (0, pad))
    wgt = (lax.dynamic_slice_in_dim(area, start, pts, 0) * valid)[:, None] * var_weight[None, :]
    aim = jnp.pad(lax.dynamic_slice_in_dim(targets, start, pts, 1).T, ((0, 0), (0, pad)))
    w_out_p = jnp.pad(w_out, ((0, 0), (0, pad)))
    b_out_p = jnp.pad(b_out, (0, pad))[None]

    pick, pick_t, aim, wgt = lax.optimization_barrier((pick, pick_t, aim, wgt))
    feats_t, hidden, slope, pred = forward(
        pick, own, swapped, same, diag, w_in, b_in[None], w_out_p, b_out_p
    )
    pred = a2a(pred, GROUP)
    dpred, small = crps(pred, aim, wgt)
    dpred = a2a(dpred, GROUP).reshape(MEMBERS * pts, LANES)
    dpre, send = backward(core, dpred, w_out_p, slope, hidden, feats_t, small)
    got = lax.ppermute(send, "c", [(0, 1), (1, 0)])
    d_own, d_swap, d_same, d_diag = latent_grads(dpre, w_in, pick_t)
    got, d_own = lax.optimization_barrier((got, d_own))
    part = pair_sum(core, dpred, dpre, hidden, feats_t, small, got)
    y = lax.axis_index("y")
    up, down = jnp.logical_and(y == 3, h == 0), jnp.logical_and(y == 0, h == 1)
    same_crosses = jnp.logical_or(up, down)
    up, down = jnp.logical_and(y == 3, h == 1), jnp.logical_and(y == 0, h == 0)
    diag_crosses = jnp.logical_or(up, down)
    crossed = lax.ppermute(jnp.where(same_crosses, d_same, d_diag), GRID, CARRY)
    d_same = jnp.where(same_crosses, crossed, d_same)
    d_diag = jnp.where(diag_crosses, crossed, d_diag)
    part = a2a(part, PLANE)
    part, d_swap, d_same, d_diag = lax.optimization_barrier((part, d_swap, d_same, d_diag))
    r_swap = lax.ppermute(d_swap, GRID, back(SWAP))
    r_same = lax.ppermute(d_same, GRID, BACK_SAME)
    r_diag = lax.ppermute(d_diag, GRID, BACK_DIAG)
    def planes(x):
        x = a2a(total_and_spread(group, x, 8), "z")
        return a2a(total_and_spread(group, x, PARTS), PLANE)

    part = lax.cond(counts[0] >= 0, planes, lambda x: x, part)
    part, r_swap, r_same, r_diag = lax.optimization_barrier((part, r_swap, r_same, r_diag))
    got = lax.ppermute(part, "c", [(0, 1), (1, 0)])
    grad_latent = final_latents(side, d_own, r_same, r_swap, r_diag)
    first = unpack(core, part)
    gw_in, gw_out_t, gb_in, gb_out, loss = unpack(1 - core, got, first)
    return (
        grad_latent,
        gw_in,
        gb_in[0],
        gw_out_t.T,
        gb_out[0],
        loss[0, 0],
    )


def solution(mesh):
    fine = Mesh(mesh.devices.reshape(2, 2, 8, 4, 2), ENS + GRID)
    in_specs = (
        P(ENS, GRID, None),
        P(GRID, None),
        P(),
        P(None, GRID),
        P(GRID),
        P(),
        P(),
        P(),
        P(),
        P(),
    )
    out_specs = (P(ENS, GRID, None), P(), P(), P(), P(), P())
    return jax.shard_map(body, mesh=fine, in_specs=in_specs, out_specs=out_specs, check_vma=False)
```
